128 devices in a mesh: gx: 4 (over y), gy: 8 (over x, core), gz: 4 (over z).
Axes of the slice: x: 4, y: 4, z: 4, core: 2. Of those that a mesh axis runs over, the one named last changes fastest.
Arguments:
- coefficients: bfloat16 [2048, 49, 128], P(('gx', 'gy', 'gz')), may hold values from -6 to 6
- send_list: int32 [3328, 2], P(('gx', 'gy', 'gz')), may hold values from 0 to 15
- sources: int32 [26624], P(('gx', 'gy', 'gz')), may hold values from 0 to 67
- targets: int32 [26624], P(('gx', 'gy', 'gz')), may hold values from 0 to 15
- wigner: bfloat16 [26624, 455], P(('gx', 'gy', 'gz')), may hold values from -4 to 4
- edge_weight: float32 [26624], P(('gx', 'gy', 'gz')), may hold values from 0.25 to 1
- cotangent: bfloat16 [2048, 49, 128], P(('gx', 'gy', 'gz')), may hold values from -0.59765625 to 0.59765625
- w_zero: bfloat16 [896, 896], replicated, may hold values from -0.1875 to 0.1875
- w_one: bfloat16 [768, 1536], replicated, may hold values from -0.21875 to 0.21875
- w_two: bfloat16 [640, 1280], replicated, may hold values from -0.25 to 0.25
Outputs:
- updated: bfloat16 [2048, 49, 128], P(('gx', 'gy', 'gz'))
- grad_coefficients: float32 [2048, 49, 128], P(('gx', 'gy', 'gz'))
- grad_zero: float32 [802816], P(('gx', 'gy', 'gz'))
- grad_one: float32 [1179648], P(('gx', 'gy', 'gz'))
- grad_two: float32 [819200], P(('gx', 'gy', 'gz'))
The draws below stay inside these ranges and needn't reach their ends.
All inputs are finite; a program needn't handle non-finite values.
Results may differ from the reference program's by a relative error of at most 0.006.
Values may be sent and summed in bfloat16 or wider, within the bound.
No kernel may reach another device: no remote copies, remote signals or barrier semaphores. Data moves between devices by JAX's collectives and lax.ppermute only.
A program may use at most 128 MiB of HBM per device.

```python
import math
import jax
import jax.numpy as jnp
import numpy as np
from jax import lax

C = 128
NBR = 13
ATOM_DEV = 16
GHOST = 2
SLOTS = 68
ATOMS = 2048
EDGES = 26624
N_GX = 4
N_GY = 8
N_GZ = 4


def draw_wigner(key, part):
    key = jax.random.fold_in(key, 11)
    degree_scales = np.concatenate([np.full((2 * d + 1) ** 2, (2 * d + 1) ** (-0.5)) for d in range(7)]).astype(np.float32)
    values = jnp.clip(jax.random.normal(key, (EDGES, 455), jnp.float32), -4.0, 4.0)
    return (values * jnp.asarray(degree_scales)).astype(jnp.bfloat16)


def with_ends(entries, rng, least, high):
    index_at = [jax.random.randint(jax.random.fold_in(rng, axis), (), 0, length) for axis, length in enumerate(entries.shape)]
    main_axis = entries.shape.index(max(entries.shape))
    next_to = index_at[:main_axis] + [(index_at[main_axis] + 1) % entries.shape[main_axis]] + index_at[main_axis + 1:]
    return entries.at[tuple(index_at)].set(least).at[tuple(next_to)].set(high)


def steps_of(key, dims, cuts, smallest, top_value):
    def one(axis_at, blocks):
        draws = jax.random.uniform(jax.random.fold_in(jax.random.fold_in(key, 6), axis_at), (blocks,), jnp.float32, smallest / len(cuts), top_value / len(cuts))
        return jnp.repeat(jnp.exp(draws), dims[axis_at] // blocks).reshape((-1,) + (1,) * (len(dims) - axis_at - 1))

    gain = one(*cuts[0])
    for cut in cuts[1:]:
        gain = gain * one(*cut)
    return gain


def normal_values(stream_key, shape, scale, limit, shards=(), held_as=jnp.bfloat16):
    entries = jax.random.normal(stream_key, shape, jnp.float32) * scale
    if len(shards) > 0:
        entries = steps_of(stream_key, shape, shards, -0.22, 0.18) * entries
    return jnp.clip(entries, min=-limit, max=limit).astype(held_as)


def setup_inputs(seed: int = 0) -> dict:
    streams_of = jax.random.split(jax.random.key(seed), 11)
    coefficients = normal_values(streams_of[0], (ATOMS, 49, C), 1.0, 6.0, ((0, 128),))
    send_list = with_ends(jax.random.randint(streams_of[1], (26 * N_GX * N_GY * N_GZ, GHOST), 0, ATOM_DEV), jax.random.fold_in(streams_of[1], 1), 0, ATOM_DEV - 1).astype(jnp.int32)
    sources = with_ends(jax.random.randint(streams_of[2], (EDGES,), 0, SLOTS), jax.random.fold_in(streams_of[2], 1), 0, SLOTS - 1).astype(jnp.int32)
    targets = with_ends(jax.random.randint(streams_of[3], (EDGES,), 0, ATOM_DEV), jax.random.fold_in(streams_of[3], 1), 0, ATOM_DEV - 1).astype(jnp.int32)
    wigner = draw_wigner(jax.random.fold_in(streams_of[10], 71), 0)
    edge_weight = jnp.clip(jnp.exp(math.log(1.0) - 1.3862944 * jax.random.uniform(streams_of[5], (EDGES,), jnp.float32) ** steps_of(streams_of[5], (EDGES,), ((0, 128),), -0.2, 0.2)), 0.25, 1.0)
    cotangent = normal_values(streams_of[6], (ATOMS, 49, C), 0.1, 0.59765625, ((0, 128),))
    w_zero = normal_values(streams_of[7], (7 * C, 7 * C), (7 * C) ** -0.5, 0.1875)
    w_one = normal_values(streams_of[8], (6 * C, 12 * C), (6 * C) ** -0.5, 0.21875)
    w_two = normal_values(streams_of[9], (5 * C, 10 * C), (5 * C) ** -0.5, 0.25)
    return {"coefficients": coefficients, "send_list": send_list, "sources": sources, "targets": targets, "wigner": wigner, "edge_weight": edge_weight, "cotangent": cotangent, "w_zero": w_zero, "w_one": w_one, "w_two": w_two}


block_starts = [0, 1, 10, 35, 84, 165, 286, 455]


def rotation_block(wigner, degree):
    span_size = 2 * degree + 1
    kept_rows = min(degree, 2)
    rotation = wigner[:, block_starts[degree]:block_starts[degree + 1]].reshape(-1, span_size, span_size)
    return rotation[:, degree - kept_rows:degree + kept_rows + 1, :].astype(jnp.float32)


def rotate_in(wigner, features):
    pieces = []
    for degree in range(7):
        slab_part = features[:, degree * degree:(degree + 1) * (degree + 1), :].astype(jnp.float32)
        pieces.append(jnp.einsum("eij,ejc->eic", rotation_block(wigner, degree), slab_part))
    return pieces


def rotate_out(wigner, pieces):
    outputs = [jnp.einsum("eij,eic->ejc", rotation_block(wigner, degree), pieces[degree].astype(jnp.float32), precision=lax.Precision.HIGHEST) for degree in range(7)]
    return jnp.concatenate(outputs, axis=1)


def split_orders(pieces):
    count = pieces[0].shape[0]
    zeroth = jnp.stack([pieces[d][:, min(d, 2)] for d in range(7)], 1).reshape(count, -1)
    plus_one = jnp.stack([pieces[d][:, min(d, 2) + 1] for d in range(1, 7)], 1).reshape(count, -1)
    minus_one = jnp.stack([pieces[d][:, min(d, 2) - 1] for d in range(1, 7)], 1).reshape(count, -1)
    plus_two = jnp.stack([pieces[d][:, 4] for d in range(2, 7)], 1).reshape(count, -1)
    minus_two = jnp.stack([pieces[d][:, 0] for d in range(2, 7)], 1).reshape(count, -1)
    return zeroth, plus_one, minus_one, plus_two, minus_two


def join_orders(orders, channels):
    count = orders[0].shape[0]
    zeroth = orders[0].reshape(count, 7, channels)
    plus_one = orders[1].reshape(count, 6, channels)
    minus_one = orders[2].reshape(count, 6, channels)
    plus_two = orders[3].reshape(count, 5, channels)
    minus_two = orders[4].reshape(count, 5, channels)
    pieces = [zeroth[:, 0:1]]
    pieces.append(jnp.stack([minus_one[:, 0], zeroth[:, 1], plus_one[:, 0]], 1))
    for degree in range(2, 7):
        pieces.append(jnp.stack([minus_two[:, degree - 2], minus_one[:, degree - 1], zeroth[:, degree], plus_one[:, degree - 1], plus_two[:, degree - 2]], 1))
    return pieces


def matmul(left, right):
    return jnp.dot(left, right, preferred_element_type=jnp.float32)


def times_transposed(left, right):
    return lax.dot_general(left, right, (((1,), (1,)), ((), ())), preferred_element_type=jnp.float32)


def contract_rows(left, right):
    return lax.dot_general(left, right, (((0,), (0,)), ((), ())), preferred_element_type=jnp.float32)


def pair_forward(plus_part, minus_part, weight):
    count, span_size = plus_part.shape
    product = matmul(jnp.concatenate([plus_part, minus_part], 0), weight)
    upper_rows, lower_rows = product[:count], product[count:]
    return upper_rows[:, :span_size] - lower_rows[:, span_size:], lower_rows[:, :span_size] + upper_rows[:, span_size:]


def pair_backward(plus_part, minus_part, plus_grad, minus_grad, weight):
    count = plus_part.shape[0]
    stacked = jnp.concatenate([jnp.concatenate([plus_grad, minus_grad], 1), jnp.concatenate([minus_grad, -plus_grad], 1)], 0)
    inputs = times_transposed(stacked, weight)
    weight_grad = contract_rows(jnp.concatenate([plus_part, minus_part], 0), stacked)
    return inputs[:count], inputs[count:], weight_grad


def local_pass(slot_table, sources, targets, wigner, edge_weight, cotangent, w_zero, w_one, w_two):
    channels = slot_table.shape[2]
    own_rows = cotangent.shape[0]
    scale = edge_weight[:, None]
    orders = [o.astype(jnp.bfloat16) for o in split_orders(rotate_in(wigner, slot_table[sources]))]
    zeroth = matmul(orders[0], w_zero) * scale
    plus_one, minus_one = pair_forward(orders[1], orders[2], w_one)
    plus_two, minus_two = pair_forward(orders[3], orders[4], w_two)
    outgoing = (zeroth, plus_one * scale, minus_one * scale, plus_two * scale, minus_two * scale)
    messages = rotate_out(wigner, join_orders(outgoing, channels))
    summed = jax.ops.segment_sum(messages, targets, own_rows)
    grads = [(o * scale).astype(jnp.bfloat16) for o in split_orders(rotate_in(wigner, cotangent[targets]))]
    grad_zero = contract_rows(orders[0], grads[0])
    back_zero = times_transposed(grads[0], w_zero)
    back_plus1, back_minus1, grad_one = pair_backward(orders[1], orders[2], grads[1], grads[2], w_one)
    back_plus2, back_minus2, grad_two = pair_backward(orders[3], orders[4], grads[3], grads[4], w_two)
    returned = rotate_out(wigner, join_orders((back_zero, back_plus1, back_minus1, back_plus2, back_minus2), channels))
    slot_grads = jax.ops.segment_sum(returned, sources, slot_table.shape[0])
    return summed, slot_grads, grad_zero, grad_one, grad_two


def direction_tables():
    offsets = []
    for first in range(3):
        for second in range(3):
            for third in range(3):
                if (first, second, third) != (1, 1, 1):
                    offsets.append((first - 1, second - 1, third - 1))
    opposite = [offsets.index((-a, -b, -c)) for (a, b, c) in offsets]
    return np.array(offsets, dtype=np.int32), np.array(opposite, dtype=np.int32)


def reference(coefficients, send_list, sources, targets, wigner, edge_weight, cotangent, w_zero, w_one, w_two):
    offsets, opposite = direction_tables()
    shift_x = jnp.asarray(offsets[:, 0])
    shift_y = jnp.asarray(offsets[:, 1])
    shift_z = jnp.asarray(offsets[:, 2])
    opposite = jnp.asarray(opposite)
    domains = N_GX * N_GY * N_GZ
    edges_dev = ATOM_DEV * NBR

    def visit(carry, domain):
        summed_all, grad_all, acc_zero, acc_one, acc_two = carry
        pos_x = domain // (N_GY * N_GZ)
        pos_y = (domain // N_GZ) % N_GY
        pos_z = domain % N_GZ
        neighbour = ((pos_x + shift_x) % N_GX) * (N_GY * N_GZ) + ((pos_y + shift_y) % N_GY) * N_GZ + (pos_z + shift_z) % N_GZ
        listed = send_list[(neighbour * 26 + opposite).astype(jnp.int32)]
        ghost_ids = (neighbour[:, None] * ATOM_DEV + listed).reshape(-1).astype(jnp.int32)
        own_ids = (domain * ATOM_DEV + jnp.arange(ATOM_DEV)).astype(jnp.int32)
        all_ids = jnp.concatenate([own_ids, ghost_ids])
        slot_table = coefficients[all_ids]
        start = (domain * edges_dev).astype(jnp.int32)
        summed, slot_grads, grad_zero, grad_one, grad_two = local_pass(
            slot_table,
            lax.dynamic_slice_in_dim(sources, start, edges_dev),
            lax.dynamic_slice_in_dim(targets, start, edges_dev),
            lax.dynamic_slice_in_dim(wigner, start, edges_dev),
            lax.dynamic_slice_in_dim(edge_weight, start, edges_dev),
            lax.dynamic_slice_in_dim(cotangent, (domain * ATOM_DEV).astype(jnp.int32), ATOM_DEV),
            w_zero, w_one, w_two)
        summed_all = lax.dynamic_update_slice_in_dim(summed_all, summed, (domain * ATOM_DEV).astype(jnp.int32), 0)
        grad_all = grad_all.at[all_ids].add(slot_grads)
        return (summed_all, grad_all, acc_zero + grad_zero, acc_one + grad_one, acc_two + grad_two), None

    start_carry = (jnp.zeros(coefficients.shape, jnp.float32), jnp.zeros(coefficients.shape, jnp.float32),
                   jnp.zeros(w_zero.shape, jnp.float32), jnp.zeros(w_one.shape, jnp.float32), jnp.zeros(w_two.shape, jnp.float32))
    final, _ = lax.scan(visit, start_carry, jnp.arange(domains).astype(jnp.int32))
    summed_all, grad_all, acc_zero, acc_one, acc_two = final
    return summed_all.astype(jnp.bfloat16), grad_all, acc_zero.reshape(-1), acc_one.reshape(-1), acc_two.reshape(-1)
```

```python
import functools

import jax
import jax.numpy as jnp
from jax import lax
from jax.experimental import pallas as pl
from jax.experimental.pallas import tpu as pltpu
from jax.sharding import Mesh
from jax.sharding import PartitionSpec as P

F32 = jnp.float32
BF16 = jnp.bfloat16

LMAX = 6
ROWS = 49
C = 128
OWN = 16
CELLS = 54
TAB = 80
EDGES = 208
EPAD = 256
PITCH = 56
STARTS = [0, 1, 10, 35, 84, 165, 286, 455]

KEPT = [list(range(-min(l, 2), min(l, 2) + 1)) for l in range(LMAX + 1)]
PAIR_AT = {}
for _l in range(LMAX + 1):
    for _m in KEPT[_l]:
        PAIR_AT[(_l, _m)] = len(PAIR_AT)
PAIRS = len(PAIR_AT)
FIRST = {0: 0, 1: 7, -1: 13, 2: 19, -2: 24}


def order_block(l, m):
    return FIRST[m] + l - abs(m)


PIECE = 176
VMEM_LIMIT = 56 * 1024 * 1024


def nt(left, right):
    return lax.dot_general(left, right, (((1,), (1,)), ((), ())), preferred_element_type=F32)


def mm(left, right):
    return jnp.dot(left, right, preferred_element_type=F32)


def eye(rows, columns, dtype=BF16):
    a = lax.broadcasted_iota(jnp.int32, (rows, columns), 0)
    b = lax.broadcasted_iota(jnp.int32, (rows, columns), 1)
    return (a == b).astype(F32).astype(dtype)


def one_hot_rows(index_row, rows, out_ref):
    a = lax.broadcasted_iota(jnp.int32, (rows, EDGES), 0)
    out_ref[...] = jnp.zeros(out_ref.shape, out_ref.dtype)
    out_ref[:, :EDGES] = (a == index_row).astype(F32).astype(BF16)


def slots_of(sources_row):
    return sources_row + jnp.where(sources_row >= OWN + 26, 2, 0)


def fill_masked(wt_ref, hot_ref, l, m, out_ref, column):
    rows = hot_ref.shape[0]
    width = 2 * l + 1
    for j in range(width):
        at = STARTS[l] + (l + m) * width + j
        row = jnp.broadcast_to(wt_ref[at : at + 1, :], (16, EPAD)).astype(BF16)
        for g in range(0, rows, 16):
            out_ref[j * rows + g : j * rows + g + 16, column : column + EPAD] = (
                hot_ref[g : g + 16, :] * row
            )


def transposed_tables(flat_ref, perm_ref, slots):
    for j in range(ROWS):
        perm_ref[j * slots : (j + 1) * slots, :] = flat_ref[
            pl.ds(j, slots, stride=PITCH), :
        ].astype(BF16)
    unit = eye(C, C)
    tables = []
    for l in range(LMAX + 1):
        tables.append(
            nt(unit, perm_ref[l * l * slots : (l + 1) * (l + 1) * slots, :]).astype(BF16)
        )
    return tables


def pick_kernel(list_ref, coef_ref, minus_ref, mid_ref, plus_ref):
    outs = (minus_ref, mid_ref, plus_ref)
    for x in range(3):
        for y in range(3):
            for z in range(3):
                cell = (x * 3 + y) * 3 + z
                for a in range(2):
                    if cell == 13:
                        outs[z][x, y, a] = jnp.zeros((ROWS, C), BF16)
                    else:
                        k = cell if cell < 13 else cell - 1
                        outs[z][x, y, a] = coef_ref[list_ref[k * 2 + a]]


def q_kernel(wig_ref, tgt_ref, ew_ref, cot_ref, wt_ref, q0_ref, q1_ref, q2_ref,
             pad_ref, hot_ref, ewr_ref, flat_ref, perm_ref, a_ref, qt_ref):
    pad_ref[...] = jnp.zeros(pad_ref.shape, BF16)
    pad_ref[:EDGES, :] = wig_ref[...]
    wt_ref[...] = nt(eye(456, 455), pad_ref[...])
    one_hot_rows(tgt_ref[...], OWN, hot_ref)
    ewr_ref[...] = jnp.zeros(ewr_ref.shape, F32)
    ewr_ref[:, :EDGES] = jnp.broadcast_to(ew_ref[...], (8, EDGES))
    for a in range(OWN):
        flat_ref[a * PITCH : a * PITCH + ROWS, :] = cot_ref[a].astype(F32)
    tables = transposed_tables(flat_ref, perm_ref, OWN)
    scale = ewr_ref[0:1, :]
    for l in range(LMAX + 1):
        for m in KEPT[l]:
            fill_masked(wt_ref, hot_ref, l, m, a_ref, 0)
            q = mm(tables[l], a_ref[: (2 * l + 1) * OWN, :]) * scale
            b = order_block(l, m)
            qt_ref[b * C : (b + 1) * C, :] = q.astype(BF16)
    unit = eye(EPAD, EPAD)
    q0_ref[...] = nt(unit, qt_ref[0:896, :]).astype(BF16)
    for out, start, n in ((q1_ref, 896, 768), (q2_ref, 2432, 640)):
        plus = nt(unit, qt_ref[start : start + n, :]).astype(BF16)
        minus = nt(unit, qt_ref[start + n : start + 2 * n, :]).astype(BF16)
        out[0:EPAD, 0:n] = plus
        out[0:EPAD, n : 2 * n] = minus
        out[EPAD : 2 * EPAD, 0:n] = minus
        out[EPAD : 2 * EPAD, n : 2 * n] = -plus


def dv_kernel(q0_ref, q1_ref, q2_ref, w0_ref, w1_ref, w2_ref, dv_ref):
    def put(value, l, m):
        b = PAIR_AT[(l, m)]
        dv_ref[b * EPAD : (b + 1) * EPAD, :] = value.astype(BF16)

    for l in range(0, 7):
        put(nt(q0_ref[...], w0_ref[l * C : (l + 1) * C, :]), l, 0)
    for l in range(1, 7):
        both = nt(q1_ref[...], w1_ref[(l - 1) * C : l * C, :])
        put(both[:EPAD], l, 1)
        put(both[EPAD:], l, -1)
    for l in range(2, 7):
        both = nt(q2_ref[...], w2_ref[(l - 2) * C : (l - 1) * C, :])
        put(both[:EPAD], l, 2)
        put(both[EPAD:], l, -2)


def back_kernel(dv_ref, wt_ref, src_ref, own_ref, left_ref, mid_ref, right_ref,
                hot_ref, b_ref, sum_ref):
    one_hot_rows(slots_of(src_ref[...]), TAB, hot_ref)
    for l in range(LMAX + 1):
        rows = (2 * l + 1) * TAB
        for i, m in enumerate(KEPT[l]):
            fill_masked(wt_ref, hot_ref, l, m, b_ref, i * EPAD)
        n = len(KEPT[l])
        first = PAIR_AT[(l, KEPT[l][0])] * EPAD
        sum_ref[l * l * TAB : l * l * TAB + rows, :] = mm(
            b_ref[:rows, : n * EPAD], dv_ref[first : first + n * EPAD, :]
        )
    for s in range(OWN):
        own_ref[s] = sum_ref[pl.ds(s, ROWS, stride=TAB), :]
    outs = (left_ref, mid_ref, right_ref)
    for x in range(3):
        for y in range(3):
            for z in range(3):
                for a in range(2):
                    s = OWN + ((x * 3 + y) * 3 + z) * 2 + a
                    outs[x][y, z, a] = sum_ref[pl.ds(s, ROWS, stride=TAB), :].astype(BF16)


def v_kernel(core_ref, coef_ref, left_ref, mid_ref, right_ref, wt_ref, src_ref,
             q0_ref, q1_ref, q2_ref, vt_ref, keep_ref, send_ref,
             hot_ref, flat_ref, perm_ref, b_ref, g0_ref, g1_ref, piece_ref):
    one_hot_rows(slots_of(src_ref[...]), TAB, hot_ref)
    for s in range(OWN):
        flat_ref[s * PITCH : s * PITCH + ROWS, :] = coef_ref[s].astype(F32)
    ins = (left_ref, mid_ref, right_ref)
    for x in range(3):
        for y in range(3):
            for z in range(3):
                for a in range(2):
                    s = OWN + ((x * 3 + y) * 3 + z) * 2 + a
                    flat_ref[s * PITCH : s * PITCH + ROWS, :] = ins[x][y, z, a].astype(F32)
    spare = (OWN + CELLS) * PITCH
    flat_ref[spare:, :] = jnp.zeros((TAB * PITCH - spare, C), F32)
    tables = transposed_tables(flat_ref, perm_ref, TAB)
    for l in range(LMAX + 1):
        for m in KEPT[l]:
            fill_masked(wt_ref, hot_ref, l, m, b_ref, 0)
            v = mm(tables[l], b_ref[: (2 * l + 1) * TAB, :])
            b = order_block(l, m)
            vt_ref[b * C : (b + 1) * C, :] = v.astype(BF16)
    core = core_ref[0]
    for d in range(128):
        piece_ref[d * PIECE + PIECE - 8 : (d + 1) * PIECE, :] = jnp.zeros((8, C), F32)

    def spread(block_ref, rows, offset):
        for h in range(2):
            def one(d, _):
                p = (d // 4) * 8 + (core ^ h) * 4 + d % 4
                piece_ref[pl.ds((h * 64 + d) * PIECE + offset, 8), :] = block_ref[
                    pl.ds(p * rows, 8), :
                ]
                return 0

            lax.fori_loop(0, 64, one, 0, unroll=8)

    offset = 0
    for start, n, rows, q_ref, paired in (
        (0, 896, 7, q0_ref, False),
        (896, 768, 6, q1_ref, True),
        (2432, 640, 5, q2_ref, True),
    ):
        columns = q_ref.shape[1]
        for k in range(0, columns, 256):
            width = min(256, columns - k)
            g = mm(vt_ref[start : start + n, :], q_ref[:EPAD, k : k + width])
            if paired:
                g = g + mm(
                    vt_ref[start + n : start + 2 * n, :], q_ref[EPAD:, k : k + width]
                )
            g0_ref[:n, :] = g[:, :C]
            spread(g0_ref, rows, offset)
            offset += rows
            if width == 256:
                g1_ref[:n, :] = g[:, C:]
                spread(g1_ref, rows, offset)
                offset += rows

    def convert(d, _):
        keep_ref[d] = piece_ref[pl.ds(pl.multiple_of(d * PIECE, 16), PIECE), :].astype(BF16)
        send_ref[d] = piece_ref[
            pl.ds(pl.multiple_of((64 + d) * PIECE, 16), PIECE), :
        ].astype(BF16)
        return 0

    lax.fori_loop(0, 64, convert, 0, unroll=2)


def u_kernel(vt_ref, w0_ref, w1_ref, w2_ref, ew_ref, tgt_ref, wt_ref, out_ref,
             hot_ref, ewr_ref, v_ref, u_ref, a_ref, sum_ref):
    one_hot_rows(tgt_ref[...], OWN, hot_ref)
    ewr_ref[...] = jnp.zeros(ewr_ref.shape, F32)
    ewr_ref[:, :EDGES] = jnp.broadcast_to(ew_ref[...], (C, EDGES))
    scale = ewr_ref[...].T
    unit = eye(EPAD, EPAD)

    def put(value, l, m):
        b = PAIR_AT[(l, m)]
        u_ref[b * EPAD : (b + 1) * EPAD, :] = (value * scale).astype(BF16)

    v0 = nt(unit, vt_ref[0:896, :]).astype(BF16)
    u0 = mm(v0, w0_ref[...])
    for l in range(7):
        put(u0[:, l * C : (l + 1) * C], l, 0)
    for order, start, n, w_ref in ((1, 896, 768, w1_ref), (2, 2432, 640, w2_ref)):
        v_ref[:EPAD, :n] = nt(unit, vt_ref[start : start + n, :]).astype(BF16)
        v_ref[EPAD:, :n] = nt(unit, vt_ref[start + n : start + 2 * n, :]).astype(BF16)
        v = v_ref[:, :n]
        for l in range(order, 7):
            k = (l - order) * C
            real = mm(v, w_ref[:, k : k + C])
            imag = mm(v, w_ref[:, n + k : n + k + C])
            put(real[:EPAD] - imag[EPAD:], l, order)
            put(real[EPAD:] + imag[:EPAD], l, -order)
    for l in range(LMAX + 1):
        rows = (2 * l + 1) * OWN
        for i, m in enumerate(KEPT[l]):
            fill_masked(wt_ref, hot_ref, l, m, a_ref, i * EPAD)
        n = len(KEPT[l])
        first = PAIR_AT[(l, KEPT[l][0])] * EPAD
        sum_ref[l * l * OWN : l * l * OWN + rows, :] = mm(
            a_ref[:rows, : n * EPAD], u_ref[first : first + n * EPAD, :]
        )
    for a in range(OWN):
        out_ref[a] = sum_ref[pl.ds(a, ROWS, stride=OWN), :].astype(BF16)


def total_kernel(in_ref, zero_ref, one_ref, two_ref, acc_ref):
    def add(d, total):
        return total + in_ref[d].astype(F32)

    acc_ref[...] = lax.fori_loop(1, 64, add, in_ref[0].astype(F32), unroll=7)
    offset = 0
    for out, rows, blocks in ((zero_ref, 7, 7), (one_ref, 6, 12), (two_ref, 5, 10)):
        for t in range(rows):
            out[t * blocks : (t + 1) * blocks, :] = acc_ref[
                pl.ds(offset + t, blocks, stride=rows), :
            ]
        offset += rows * blocks


def owner_kernel(list_ref, own_ref, minus_ref, mid_ref, plus_ref, out_ref):
    out_ref[...] = own_ref[...]
    ins = (minus_ref, mid_ref, plus_ref)
    for x in range(3):
        for y in range(3):
            for z in range(3):
                cell = (x * 3 + y) * 3 + z
                if cell == 13:
                    continue
                k = cell if cell < 13 else cell - 1
                for a in range(2):
                    at = list_ref[k * 2 + a]
                    out_ref[at] = out_ref[at] + ins[z][x, y, a].astype(F32)


def call(kernel, outs, scratch=(), scalars=0, inputs=0, flops=0, moved=0):
    specs = [pl.BlockSpec(memory_space=pltpu.SMEM)] * scalars
    specs += [pl.BlockSpec(memory_space=pltpu.VMEM)] * inputs
    return pl.pallas_call(
        kernel,
        out_shape=[jax.ShapeDtypeStruct(s, d) for s, d in outs],
        in_specs=specs,
        out_specs=[pl.BlockSpec(memory_space=pltpu.VMEM)] * len(outs),
        scratch_shapes=[pltpu.VMEM(s, d) for s, d in scratch],
        compiler_params=pltpu.CompilerParams(vmem_limit_bytes=VMEM_LIMIT),
        cost_estimate=pl.CostEstimate(flops=flops, bytes_accessed=moved, transcendentals=0),
    )


def shift(value, axis, step):
    count = lax.axis_size(axis)
    return lax.ppermute(value, axis, [(i, (i + step) % count) for i in range(count)])


AXES = ("gx", "gyx", "gyc", "gz")
GY = ("gyx", "gyc")
FACE = (3, 3, 2, ROWS, C)


def regroup(parts, index, axis):
    return jnp.stack([lax.index_in_dim(p, index, axis, keepdims=False) for p in parts], 1)


def body(coefficients, send_list, sources, targets, wigner, edge_weight, cotangent, w_zero, w_one, w_two):
    listed = send_list.reshape(-1)
    src = sources.reshape(1, EDGES)
    tgt = targets.reshape(1, EDGES)
    ew = edge_weight.reshape(1, EDGES)
    core = lax.axis_index("gyc").astype(jnp.int32).reshape(1)

    z_minus, z_mid, z_plus = call(pick_kernel, [(FACE, BF16)] * 3, scalars=1, inputs=1)(
        listed, coefficients
    )
    by_z = (shift(z_plus, "gz", 1), z_mid, shift(z_minus, "gz", -1))
    by_y = (
        shift(regroup(by_z, 2, 1), GY, 1),
        regroup(by_z, 1, 1),
        shift(regroup(by_z, 0, 1), GY, -1),
    )
    take_x = lambda i: jnp.stack([p[i] for p in by_y], 0)
    left, mid, right = shift(take_x(2), "gx", 1), take_x(1), shift(take_x(0), "gx", -1)

    wt, q0, q1, q2 = call(
        q_kernel,
        [((456, EPAD), F32), ((EPAD, 896), BF16), ((512, 1536), BF16), ((512, 1280), BF16)],
        [((EPAD, 455), BF16), ((OWN, EPAD), BF16), ((8, EPAD), F32), ((OWN * PITCH, C), F32),
         ((ROWS * OWN, C), BF16), ((13 * OWN, EPAD), BF16), ((3712, EPAD), BF16)],
        inputs=4, flops=2 * 10**9, moved=8 * 10**6,
    )(wigner, tgt, ew, cotangent)
    (dv,) = call(
        dv_kernel, [((PAIRS * EPAD, C), BF16)], inputs=6, flops=3 * 10**9, moved=16 * 10**6
    )(q0, q1, q2, w_zero, w_one, w_two)
    own, g_left, g_mid, g_right = call(
        back_kernel,
        [((OWN, ROWS, C), F32)] + [(FACE, BF16)] * 3,
        [((TAB, EPAD), BF16), ((13 * TAB, 5 * EPAD), BF16), ((ROWS * TAB, C), F32)],
        inputs=3, flops=3 * 10**9, moved=12 * 10**6,
    )(dv, wt, src)

    vt, keep, send = call(
        v_kernel,
        [((3712, EPAD), BF16), ((64, PIECE, C), BF16), ((64, PIECE, C), BF16)],
        [((TAB, EPAD), BF16), ((TAB * PITCH, C), F32), ((ROWS * TAB, C), BF16),
         ((13 * TAB, EPAD), BF16), ((904, C), F32), ((904, C), F32), ((128 * PIECE, C), F32)],
        scalars=1, inputs=9, flops=4 * 10**9, moved=24 * 10**6,
    )(core, coefficients, left, mid, right, wt, src, q0, q1, q2)
    pair = keep.astype(F32) + shift(send, "gyc", 1).astype(F32)
    pieces = lax.all_to_all(pair.astype(BF16), ("gx", "gyx", "gz"), 0, 0, tiled=False)

    (updated,) = call(
        u_kernel,
        [((OWN, ROWS, C), BF16)],
        [((OWN, EPAD), BF16), ((C, EPAD), F32), ((2 * EPAD, 768), BF16),
         ((PAIRS * EPAD, C), BF16), ((13 * OWN, 5 * EPAD), BF16), ((ROWS * OWN, C), F32)],
        inputs=7, flops=4 * 10**9, moved=20 * 10**6,
    )(vt, w_zero, w_one, w_two, ew, tgt, wt)
    by_x = (shift(g_right, "gx", 1), g_mid, shift(g_left, "gx", -1))
    take_y = lambda i: jnp.stack([p[i] for p in by_x], 0)
    by_y = (shift(take_y(2), GY, 1), take_y(1), shift(take_y(0), GY, -1))
    take_z = lambda i: regroup(by_y, i, 1)
    b_minus, b_mid, b_plus = shift(take_z(2), "gz", 1), take_z(1), shift(take_z(0), "gz", -1)
    (gradient,) = call(owner_kernel, [((OWN, ROWS, C), F32)], scalars=1, inputs=4)(
        listed, own, b_minus, b_mid, b_plus
    )
    zero, one, two = call(
        total_kernel,
        [((49, C), F32), ((72, C), F32), ((50, C), F32)],
        [((PIECE, C), F32)],
        inputs=1, flops=10**7, moved=4 * 10**6,
    )(pieces)
    return updated, gradient, zero.reshape(-1), one.reshape(-1), two.reshape(-1)


def solution(mesh):
    gx, gy, gz = mesh.devices.shape
    split = Mesh(mesh.devices.reshape(gx, gy // 2, 2, gz), AXES)
    lead = lambda rank: P(AXES, *([None] * (rank - 1)))
    in_specs = (lead(3), lead(2), lead(1), lead(1), lead(2), lead(1), lead(3), P(), P(), P())
    out_specs = (lead(3), lead(3), lead(1), lead(1), lead(1))
    return jax.shard_map(body, mesh=split, in_specs=in_specs, out_specs=out_specs, check_vma=False)
```

```python
import functools

import jax
import jax.numpy as jnp
from jax import lax
from jax.experimental import pallas as pl
from jax.experimental.pallas import tpu as pltpu
from jax.sharding import Mesh
from jax.sharding import PartitionSpec as P

F32 = jnp.float32
BF16 = jnp.bfloat16

LMAX = 6
ROWS = 49
C = 128
OWN = 16
CELLS = 54
TAB = 80
EDGES = 208
EPAD = 256
PITCH = 56
STARTS = [0, 1, 10, 35, 84, 165, 286, 455]

KEPT = [list(range(-min(l, 2), min(l, 2) + 1)) for l in range(LMAX + 1)]
PAIR_AT = {}
for _l in range(LMAX + 1):
    for _m in KEPT[_l]:
        PAIR_AT[(_l, _m)] = len(PAIR_AT)
PAIRS = len(PAIR_AT)
FIRST = {0: 0, 1: 7, -1: 13, 2: 19, -2: 24}


def order_block(l, m):
    return FIRST[m] + l - abs(m)


PIECE = 176
VMEM_LIMIT = 56 * 1024 * 1024


def nt(left, right):
    return lax.dot_general(left, right, (((1,), (1,)), ((), ())), preferred_element_type=F32)


def mm(left, right):
    return jnp.dot(left, right, preferred_element_type=F32)


def eye(rows, columns, dtype=BF16):
    a = lax.broadcasted_iota(jnp.int32, (rows, columns), 0)
    b = lax.broadcasted_iota(jnp.int32, (rows, columns), 1)
    return (a == b).astype(F32).astype(dtype)


def one_hot_rows(index_row, rows, out_ref):
    a = lax.broadcasted_iota(jnp.int32, (rows, EDGES), 0)
    out_ref[...] = jnp.zeros(out_ref.shape, out_ref.dtype)
    out_ref[:, :EDGES] = (a == index_row).astype(F32).astype(BF16)


def slots_of(sources_row):
    return sources_row + jnp.where(sources_row >= OWN + 26, 2, 0)


def fill_masked(wt_ref, hot_ref, l, m, out_ref, column):
    rows = hot_ref.shape[0]
    width = 2 * l + 1
    for j in range(width):
        at = STARTS[l] + (l + m) * width + j
        row = jnp.broadcast_to(wt_ref[at : at + 1, :], (16, EPAD)).astype(BF16)
        for g in range(0, rows, 16):
            out_ref[j * rows + g : j * rows + g + 16, column : column + EPAD] = (
                hot_ref[g : g + 16, :] * row
            )


def transposed_tables(perm_ref, slots):
    unit = eye(C, C)
    return [
        nt(unit, perm_ref[l * l * slots : (l + 1) * (l + 1) * slots, :]).astype(BF16)
        for l in range(LMAX + 1)
    ]


def pick_kernel(list_ref, coef_ref, minus_ref, mid_ref, plus_ref, flat_ref):
    flat_ref[...] = coef_ref[...].astype(F32)
    outs = (minus_ref, mid_ref, plus_ref)
    for x in range(3):
        for y in range(3):
            for z in range(3):
                cell = (x * 3 + y) * 3 + z
                for a in range(2):
                    if cell == 13:
                        outs[z][x, y, a] = jnp.zeros((ROWS, C), BF16)
                    else:
                        k = cell if cell < 13 else cell - 1
                        outs[z][x, y, a] = flat_ref[
                            pl.ds(list_ref[a, k], ROWS, stride=OWN), :
                        ].astype(BF16)


def q_kernel(wig_ref, tgt_ref, ew_ref, cot_ref, wt_ref, q0_ref, q1_ref, q2_ref,
             pad_ref, hot_ref, ewr_ref, a_ref, qt_ref):
    pad_ref[...] = jnp.zeros(pad_ref.shape, BF16)
    pad_ref[:EDGES, :] = wig_ref[...]
    wt_ref[...] = nt(eye(456, 455), pad_ref[...])
    one_hot_rows(tgt_ref[...], OWN, hot_ref)
    ewr_ref[...] = jnp.zeros(ewr_ref.shape, F32)
    ewr_ref[:, :EDGES] = jnp.broadcast_to(ew_ref[...], (8, EDGES))
    tables = transposed_tables(cot_ref, OWN)
    scale = ewr_ref[0:1, :]
    for l in range(LMAX + 1):
        for m in KEPT[l]:
            fill_masked(wt_ref, hot_ref, l, m, a_ref, 0)
            q = mm(tables[l], a_ref[: (2 * l + 1) * OWN, :]) * scale
            b = order_block(l, m)
            qt_ref[b * C : (b + 1) * C, :] = q.astype(BF16)
    unit = eye(EPAD, EPAD)
    q0_ref[...] = nt(unit, qt_ref[0:896, :]).astype(BF16)
    for out, start, n in ((q1_ref, 896, 768), (q2_ref, 2432, 640)):
        plus = nt(unit, qt_ref[start : start + n, :]).astype(BF16)
        minus = nt(unit, qt_ref[start + n : start + 2 * n, :]).astype(BF16)
        out[0:EPAD, 0:n] = plus
        out[0:EPAD, n : 2 * n] = minus
        out[EPAD : 2 * EPAD, 0:n] = minus
        out[EPAD : 2 * EPAD, n : 2 * n] = -plus


def fetch(hbm_refs, refs, sems):
    copies = [pltpu.make_async_copy(h, r, sems.at[i]) for i, (h, r) in enumerate(zip(hbm_refs, refs))]
    for copy in copies:
        copy.start()
    return copies


def dv_kernel(q0_ref, q1_ref, q2_ref, w0_hbm, w1_hbm, w2_hbm, dv_ref, w0_ref, w1_ref, w2_ref, sems):
    copies = fetch((w0_hbm, w1_hbm, w2_hbm), (w0_ref, w1_ref, w2_ref), sems)

    def put(value, l, m):
        b = PAIR_AT[(l, m)]
        dv_ref[b * EPAD : (b + 1) * EPAD, :] = value.astype(BF16)

    for order, q_ref, w_ref in ((0, q0_ref, w0_ref), (1, q1_ref, w1_ref), (2, q2_ref, w2_ref)):
        copies[order].wait()
        blocks = 7 - order
        for k in range(0, blocks, 2):
            n = min(2, blocks - k)
            both = nt(q_ref[...], w_ref[k * C : (k + n) * C, :])
            for i in range(n):
                put(both[:EPAD, i * C : (i + 1) * C], order + k + i, order)
                if order > 0:
                    put(both[EPAD:, i * C : (i + 1) * C], order + k + i, -order)


def back_kernel(dv_ref, wt_ref, src_ref, own_ref, left_ref, mid_ref, right_ref,
                hot_ref, b_ref, sum_ref):
    one_hot_rows(slots_of(src_ref[...]), TAB, hot_ref)
    for l in range(LMAX + 1):
        rows = (2 * l + 1) * TAB
        for i, m in enumerate(KEPT[l]):
            fill_masked(wt_ref, hot_ref, l, m, b_ref, i * EPAD)
        n = len(KEPT[l])
        first = PAIR_AT[(l, KEPT[l][0])] * EPAD
        sum_ref[l * l * TAB : l * l * TAB + rows, :] = mm(
            b_ref[:rows, : n * EPAD], dv_ref[first : first + n * EPAD, :]
        )
    for j in range(ROWS):
        own_ref[j * OWN : (j + 1) * OWN, :] = sum_ref[j * TAB : j * TAB + OWN, :]
    outs = (left_ref, mid_ref, right_ref)
    for x in range(3):
        for y in range(3):
            for z in range(3):
                for a in range(2):
                    s = OWN + ((x * 3 + y) * 3 + z) * 2 + a
                    outs[x][y, z, a] = sum_ref[pl.ds(s, ROWS, stride=TAB), :].astype(BF16)


def v_kernel(coef_ref, left_ref, mid_ref, right_ref, wt_ref, src_ref, v0_ref, v1_ref, v2_ref,
             hot_ref, flat_ref, perm_ref, b_ref):
    one_hot_rows(slots_of(src_ref[...]), TAB, hot_ref)
    ins = (left_ref, mid_ref, right_ref)
    for x in range(3):
        for y in range(3):
            for z in range(3):
                for a in range(2):
                    s = ((x * 3 + y) * 3 + z) * 2 + a
                    flat_ref[s * PITCH : s * PITCH + ROWS, :] = ins[x][y, z, a].astype(F32)
    flat_ref[CELLS * PITCH :, :] = jnp.zeros(((TAB - OWN - CELLS) * PITCH, C), F32)
    for j in range(ROWS):
        perm_ref[j * TAB : j * TAB + OWN, :] = coef_ref[j * OWN : (j + 1) * OWN, :]
        perm_ref[j * TAB + OWN : (j + 1) * TAB, :] = flat_ref[
            pl.ds(j, TAB - OWN, stride=PITCH), :
        ].astype(BF16)
    tables = transposed_tables(perm_ref, TAB)
    outs = {0: v0_ref, 1: v1_ref, 2: v2_ref}
    for l in range(LMAX + 1):
        for m in KEPT[l]:
            fill_masked(wt_ref, hot_ref, l, m, b_ref, 0)
            v = mm(tables[l], b_ref[: (2 * l + 1) * TAB, :]).astype(BF16)
            k = (l - abs(m)) * C
            column = EPAD if m < 0 else 0
            outs[abs(m)][k : k + C, column : column + EPAD] = v


ORDER_ROWS = {0: 7, 1: 6, 2: 5}
PART_BLOCKS = (
    [(0, k) for k in range(7)] + [(1, k) for k in range(5)],
    [(1, k) for k in range(5, 12)] + [(2, k) for k in range(10)],
)
PART_ROWS = (80, 96)
LEAD = 8
TALL = 912


def grad_kernel(part, core_ref, *refs):
    orders = sorted({o for o, _ in PART_BLOCKS[part]})
    v_refs = dict(zip(orders, refs[: len(orders)]))
    q_refs = dict(zip(orders, refs[len(orders) : 2 * len(orders)]))
    keep_ref, send_ref, g_ref = refs[2 * len(orders) :]
    blocks = PART_BLOCKS[part]
    i = 0
    while i < len(blocks):
        order, k = blocks[i]
        n = 2 if i + 1 < len(blocks) and blocks[i + 1][0] == order else 1
        g = mm(v_refs[order][...], q_refs[order][:, k * C : (k + n) * C])
        rows = g.shape[0]
        for t in range(n):
            g_ref[i + t, LEAD : LEAD + rows, :] = g[:, t * C : (t + 1) * C]
        i += n
    source = []
    for i, (order, _) in enumerate(blocks):
        source += [(i, order, t) for t in range(ORDER_ROWS[order])]
    while len(source) < PART_ROWS[part]:
        i, order, t = source[-1]
        source.append((i, order, t + 1))
    place = lax.broadcasted_iota(jnp.int32, (8, C), 0)
    core = core_ref[0]

    def eight(p, first):
        value = None
        last = None
        for s in range(8):
            i, order, t = source[first + s]
            if i == last:
                continue
            last = i
            start = p * ORDER_ROWS[order] + (LEAD + t - s)
            rows = g_ref[i, pl.ds(start, 8), :]
            value = rows if value is None else jnp.where(place >= s, rows, value)
        return value

    def one(d, _):
        for h, out in ((0, keep_ref), (1, send_ref)):
            p = (d // 4) * 8 + (core ^ h) * 4 + d % 4
            for r in range(0, PART_ROWS[part], 16):
                out[d, r : r + 16, :] = jnp.concatenate(
                    [eight(p, r), eight(p, r + 8)], 0
                ).astype(BF16)
        return 0

    lax.fori_loop(0, 64, one, 0, unroll=2)


def u_kernel(v0_ref, v1_ref, v2_ref, ew_ref, tgt_ref, wt_ref, w0_hbm, w1_hbm, w2_hbm, out_ref,
             hot_ref, ewr_ref, v_ref, u_ref, a_ref, w0_ref, w1_ref, w2_ref, sems):
    copies = fetch((w0_hbm, w1_hbm, w2_hbm), (w0_ref, w1_ref, w2_ref), sems)
    one_hot_rows(tgt_ref[...], OWN, hot_ref)
    ewr_ref[...] = jnp.zeros(ewr_ref.shape, F32)
    ewr_ref[:, :EDGES] = jnp.broadcast_to(ew_ref[...], (C, EDGES))
    scale = ewr_ref[...].T
    unit = eye(EPAD, EPAD)

    def put(value, l, m):
        b = PAIR_AT[(l, m)]
        u_ref[b * EPAD : (b + 1) * EPAD, :] = (value * scale).astype(BF16)

    v_ref[:EPAD, :] = nt(unit, v0_ref[...]).astype(BF16)
    copies[0].wait()
    for k in range(0, 7, 2):
        n = min(2, 7 - k)
        u0 = mm(v_ref[:EPAD, :], w0_ref[:, k * C : (k + n) * C])
        for i in range(n):
            put(u0[:, i * C : (i + 1) * C], k + i, 0)
    for order, vt_ref, w_ref in ((1, v1_ref, w1_ref), (2, v2_ref, w2_ref)):
        n = vt_ref.shape[0]
        v_ref[:EPAD, :n] = nt(unit, vt_ref[:, :EPAD]).astype(BF16)
        v_ref[EPAD:, :n] = nt(unit, vt_ref[:, EPAD:]).astype(BF16)
        v = v_ref[:, :n]
        copies[order].wait()
        for k in range(0, 7 - order, 2):
            c = min(2, 7 - order - k)
            real = mm(v, w_ref[:, k * C : (k + c) * C])
            imag = mm(v, w_ref[:, n + k * C : n + (k + c) * C])
            plus = real[:EPAD] - imag[EPAD:]
            minus = real[EPAD:] + imag[:EPAD]
            for i in range(c):
                put(plus[:, i * C : (i + 1) * C], order + k + i, order)
                put(minus[:, i * C : (i + 1) * C], order + k + i, -order)
    for l in range(LMAX + 1):
        rows = (2 * l + 1) * OWN
        for i, m in enumerate(KEPT[l]):
            fill_masked(wt_ref, hot_ref, l, m, a_ref, i * EPAD)
        n = len(KEPT[l])
        first = PAIR_AT[(l, KEPT[l][0])] * EPAD
        out_ref[l * l * OWN : l * l * OWN + rows, :] = mm(
            a_ref[:rows, : n * EPAD], u_ref[first : first + n * EPAD, :]
        ).astype(BF16)


def total_kernel(in_ref, zero_ref, one_ref, two_ref, acc_ref):
    def add(d, total):
        return total + in_ref[d].astype(F32)

    acc_ref[...] = lax.fori_loop(1, 64, add, in_ref[0].astype(F32), unroll=7)
    for out, rows, blocks, runs in (
        (zero_ref, 7, 7, ((0, 7, 0),)),
        (one_ref, 6, 12, ((0, 5, 49), (5, 7, 80))),
        (two_ref, 5, 10, ((0, 10, 122),)),
    ):
        for t in range(rows):
            for first, count, offset in runs:
                out[t * blocks + first : t * blocks + first + count, :] = acc_ref[
                    pl.ds(offset + t, count, stride=rows), :
                ]


def owner_kernel(list_ref, own_ref, minus_ref, mid_ref, plus_ref, out_ref):
    out_ref[...] = own_ref[...]
    ins = (minus_ref, mid_ref, plus_ref)
    for x in range(3):
        for y in range(3):
            for z in range(3):
                cell = (x * 3 + y) * 3 + z
                if cell == 13:
                    continue
                k = cell if cell < 13 else cell - 1
                for a in range(2):
                    rows = pl.ds(list_ref[a, k], ROWS, stride=OWN)
                    out_ref[rows, :] = out_ref[rows, :] + ins[z][x, y, a].astype(F32)


def call(kernel, outs, scratch=(), scalars=0, inputs=0, far=0, flops=0, moved=0):
    specs = [pl.BlockSpec(memory_space=pltpu.SMEM)] * scalars
    specs += [pl.BlockSpec(memory_space=pltpu.VMEM)] * inputs
    specs += [pl.BlockSpec(memory_space=pl.ANY)] * far
    buffers = [pltpu.VMEM(s, d) for s, d in scratch]
    if far:
        buffers.append(pltpu.SemaphoreType.DMA((far,)))
    return pl.pallas_call(
        kernel,
        out_shape=[jax.ShapeDtypeStruct(s, d) for s, d in outs],
        in_specs=specs,
        out_specs=[pl.BlockSpec(memory_space=pltpu.VMEM)] * len(outs),
        scratch_shapes=buffers,
        compiler_params=pltpu.CompilerParams(vmem_limit_bytes=VMEM_LIMIT),
        cost_estimate=pl.CostEstimate(flops=flops, bytes_accessed=moved, transcendentals=0),
    )


def shift(value, axis, step):
    count = lax.axis_size(axis)
    return lax.ppermute(value, axis, [(i, (i + step) % count) for i in range(count)])


AXES = ("gx", "gyx", "gyc", "gz")
GY = ("gyx", "gyc")
FACE = (3, 3, 2, ROWS, C)


def regroup(parts, index, axis):
    return jnp.stack([lax.index_in_dim(p, index, axis, keepdims=False) for p in parts], 1)


def by_component(atoms):
    return atoms.transpose(1, 0, 2).reshape(ROWS * OWN, C)


def by_atom(rows):
    return rows.reshape(ROWS, OWN, C).transpose(1, 0, 2)


WEIGHTS = [((896, 896), BF16), ((768, 1536), BF16), ((640, 1280), BF16)]
ORDERS = [((896, EPAD), BF16), ((768, 2 * EPAD), BF16), ((640, 2 * EPAD), BF16)]


def body(coefficients, send_list, sources, targets, wigner, edge_weight, cotangent, w_zero, w_one, w_two):
    listed = send_list.T
    src = sources.reshape(1, EDGES)
    tgt = targets.reshape(1, EDGES)
    ew = edge_weight.reshape(1, EDGES)
    core = lax.axis_index("gyc").astype(jnp.int32).reshape(1)
    coef = by_component(coefficients)

    z_minus, z_mid, z_plus = call(
        pick_kernel, [(FACE, BF16)] * 3, [((ROWS * OWN, C), F32)], scalars=1, inputs=1
    )(listed, coef)
    by_z = (shift(z_plus, "gz", 1), z_mid, shift(z_minus, "gz", -1))
    wt, q0, q1, q2 = call(
        q_kernel,
        [((456, EPAD), F32), ((EPAD, 896), BF16), ((512, 1536), BF16), ((512, 1280), BF16)],
        [((EPAD, 455), BF16), ((OWN, EPAD), BF16), ((8, EPAD), F32),
         ((13 * OWN, EPAD), BF16), ((3712, EPAD), BF16)],
        inputs=4, flops=2 * 10**9, moved=8 * 10**6,
    )(wigner, tgt, ew, by_component(cotangent))

    y_plus, y_minus = regroup(by_z, 2, 1), regroup(by_z, 0, 1)
    y_plus, y_minus, q0, q1, q2 = lax.optimization_barrier((y_plus, y_minus, q0, q1, q2))
    by_y = (shift(y_plus, GY, 1), regroup(by_z, 1, 1), shift(y_minus, GY, -1))
    (dv,) = call(
        dv_kernel, [((PAIRS * EPAD, C), BF16)], WEIGHTS, inputs=3, far=3,
        flops=3 * 10**9, moved=16 * 10**6,
    )(q0, q1, q2, w_zero, w_one, w_two)

    take_x = lambda i: jnp.stack([p[i] for p in by_y], 0)
    x_plus, x_minus, dv = lax.optimization_barrier((take_x(2), take_x(0), dv))
    left, mid, right = shift(x_plus, "gx", 1), take_x(1), shift(x_minus, "gx", -1)
    own, g_left, g_mid, g_right = call(
        back_kernel,
        [((ROWS * OWN, C), F32)] + [(FACE, BF16)] * 3,
        [((TAB, EPAD), BF16), ((13 * TAB, 5 * EPAD), BF16), ((ROWS * TAB, C), F32)],
        inputs=3, flops=3 * 10**9, moved=12 * 10**6,
    )(dv, wt, src)

    left, mid, right, g_left, g_right = lax.optimization_barrier((left, mid, right, g_left, g_right))
    v0, v1, v2 = call(
        v_kernel,
        ORDERS,
        [((TAB, EPAD), BF16), (((TAB - OWN) * PITCH, C), F32), ((ROWS * TAB, C), BF16),
         ((13 * TAB, EPAD), BF16)],
        inputs=6, flops=3 * 10**9, moved=8 * 10**6,
    )(coef, left, mid, right, wt, src)
    halves = []
    for part, operands in enumerate(((v0, v1, q0, q1), (v1, v2, q1, q2))):
        shape = (64, PART_ROWS[part], C)
        keep, send = call(
            functools.partial(grad_kernel, part),
            [(shape, BF16)] * 2,
            [((len(PART_BLOCKS[part]), TALL, C), F32)],
            scalars=1, inputs=4, flops=2 * 10**9, moved=12 * 10**6,
        )(core, *operands)
        halves.append((keep, shift(send, "gyc", 1)))
    pair = jnp.concatenate(
        [(k.astype(F32) + r.astype(F32)).astype(BF16) for k, r in halves], 1
    )
    pieces = lax.all_to_all(pair, ("gx", "gyx", "gz"), 0, 0, tiled=False)

    (updated,) = call(
        u_kernel,
        [((ROWS * OWN, C), BF16)],
        [((OWN, EPAD), BF16), ((C, EPAD), F32), ((2 * EPAD, 896), BF16),
         ((PAIRS * EPAD, C), BF16), ((13 * OWN, 5 * EPAD), BF16)] + WEIGHTS,
        inputs=6, far=3, flops=4 * 10**9, moved=20 * 10**6,
    )(v0, v1, v2, ew, tgt, wt, w_zero, w_one, w_two)
    by_x = (shift(g_right, "gx", 1), g_mid, shift(g_left, "gx", -1))
    take_y = lambda i: jnp.stack([p[i] for p in by_x], 0)
    by_y = (shift(take_y(2), GY, 1), take_y(1), shift(take_y(0), GY, -1))
    take_z = lambda i: regroup(by_y, i, 1)
    b_minus, b_mid, b_plus = shift(take_z(2), "gz", 1), take_z(1), shift(take_z(0), "gz", -1)
    (gradient,) = call(owner_kernel, [((ROWS * OWN, C), F32)], scalars=1, inputs=4)(
        listed, own, b_minus, b_mid, b_plus
    )
    zero, one, two = call(
        total_kernel,
        [((49, C), F32), ((72, C), F32), ((50, C), F32)],
        [((PIECE, C), F32)],
        inputs=1, flops=10**7, moved=4 * 10**6,
    )(pieces)
    return by_atom(updated), by_atom(gradient), zero.reshape(-1), one.reshape(-1), two.reshape(-1)


def solution(mesh):
    gx, gy, gz = mesh.devices.shape
    split = Mesh(mesh.devices.reshape(gx, gy // 2, 2, gz), AXES)
    lead = lambda rank: P(AXES, *([None] * (rank - 1)))
    in_specs = (lead(3), lead(2), lead(1), lead(1), lead(2), lead(1), lead(3), P(), P(), P())
    out_specs = (lead(3), lead(3), lead(1), lead(1), lead(1))
    return jax.shard_map(body, mesh=split, in_specs=in_specs, out_specs=out_specs, check_vma=False)
```

```python
import functools

import jax
import jax.numpy as jnp
from jax import lax
from jax.experimental import pallas as pl
from jax.experimental.pallas import tpu as pltpu
from jax.sharding import Mesh
from jax.sharding import PartitionSpec as P

F32 = jnp.float32
BF16 = jnp.bfloat16

LMAX = 6
ROWS = 49
C = 128
OWN = 16
CELLS = 54
TAB = 80
EDGES = 208
EPAD = 256
PITCH = 56
STARTS = [0, 1, 10, 35, 84, 165, 286, 455]

KEPT = [list(range(-min(l, 2), min(l, 2) + 1)) for l in range(LMAX + 1)]
PAIR_AT = {}
for _l in range(LMAX + 1):
    for _m in KEPT[_l]:
        PAIR_AT[(_l, _m)] = len(PAIR_AT)
PAIRS = len(PAIR_AT)
FIRST = {0: 0, 1: 7, -1: 13, 2: 19, -2: 24}


def order_block(l, m):
    return FIRST[m] + l - abs(m)


PIECE = 176
MIB = 1024 * 1024


def nt(left, right):
    return lax.dot_general(left, right, (((1,), (1,)), ((), ())), preferred_element_type=F32)


def mm(left, right):
    return jnp.dot(left, right, preferred_element_type=F32)


def eye(rows, columns, dtype=BF16):
    a = lax.broadcasted_iota(jnp.int32, (rows, columns), 0)
    b = lax.broadcasted_iota(jnp.int32, (rows, columns), 1)
    return (a == b).astype(F32).astype(dtype)


def one_hot_rows(index_row, rows, out_ref):
    a = lax.broadcasted_iota(jnp.int32, (rows, EDGES), 0)
    out_ref[...] = jnp.zeros(out_ref.shape, out_ref.dtype)
    out_ref[:, :EDGES] = (a == index_row).astype(F32).astype(BF16)


def slots_of(sources_row):
    return sources_row + jnp.where(sources_row >= OWN + 26, 2, 0)


def fill_masked(wt_ref, hot_ref, l, m, out_ref, column):
    rows = hot_ref.shape[0]
    width = 2 * l + 1
    for j in range(width):
        at = STARTS[l] + (l + m) * width + j
        row = jnp.broadcast_to(wt_ref[at : at + 1, :], (16, EPAD)).astype(BF16)
        for g in range(0, rows, 16):
            out_ref[j * rows + g : j * rows + g + 16, column : column + EPAD] = (
                hot_ref[g : g + 16, :] * row
            )


def transposed_tables(perm_ref, slots):
    unit = eye(C, C)
    return [
        nt(unit, perm_ref[l * l * slots : (l + 1) * (l + 1) * slots, :]).astype(BF16)
        for l in range(LMAX + 1)
    ]


def pick_kernel(list_ref, coef_ref, minus_ref, mid_ref, plus_ref, flat_ref):
    flat_ref[...] = coef_ref[...].astype(F32)
    outs = (minus_ref, mid_ref, plus_ref)
    for x in range(3):
        for y in range(3):
            for z in range(3):
                cell = (x * 3 + y) * 3 + z
                for a in range(2):
                    if cell == 13:
                        outs[z][x, y, a] = jnp.zeros((ROWS, C), BF16)
                    else:
                        k = cell if cell < 13 else cell - 1
                        outs[z][x, y, a] = flat_ref[
                            pl.ds(list_ref[a, k], ROWS, stride=OWN), :
                        ].astype(BF16)


def q_kernel(wig_ref, tgt_ref, ew_ref, cot_ref, wt_ref, q0_ref, q1_ref, q2_ref,
             pad_ref, hot_ref, ewr_ref, a_ref, qt_ref):
    pad_ref[...] = jnp.zeros(pad_ref.shape, BF16)
    pad_ref[:EDGES, :] = wig_ref[...]
    wt_ref[...] = nt(eye(456, 455), pad_ref[...])
    one_hot_rows(tgt_ref[...], OWN, hot_ref)
    ewr_ref[...] = jnp.zeros(ewr_ref.shape, F32)
    ewr_ref[:, :EDGES] = jnp.broadcast_to(ew_ref[...], (8, EDGES))
    tables = transposed_tables(cot_ref, OWN)
    scale = ewr_ref[0:1, :]
    for l in range(LMAX + 1):
        for m in KEPT[l]:
            fill_masked(wt_ref, hot_ref, l, m, a_ref, 0)
            q = mm(tables[l], a_ref[: (2 * l + 1) * OWN, :]) * scale
            b = order_block(l, m)
            qt_ref[b * C : (b + 1) * C, :] = q.astype(BF16)
    unit = eye(EPAD, EPAD)
    q0_ref[...] = nt(unit, qt_ref[0:896, :]).astype(BF16)
    for out, start, n in ((q1_ref, 896, 768), (q2_ref, 2432, 640)):
        plus = nt(unit, qt_ref[start : start + n, :]).astype(BF16)
        minus = nt(unit, qt_ref[start + n : start + 2 * n, :]).astype(BF16)
        out[0:EPAD, 0:n] = plus
        out[0:EPAD, n : 2 * n] = minus
        out[EPAD : 2 * EPAD, 0:n] = minus
        out[EPAD : 2 * EPAD, n : 2 * n] = -plus


def fetch(hbm_refs, refs, sems):
    copies = [pltpu.make_async_copy(h, r, sems.at[i]) for i, (h, r) in enumerate(zip(hbm_refs, refs))]
    for copy in copies:
        copy.start()
    return copies


def dv_kernel(q0_ref, q1_ref, q2_ref, w0_hbm, w1_hbm, w2_hbm, dv_ref, w0_ref, w1_ref, w2_ref, sems):
    copies = fetch((w0_hbm, w1_hbm, w2_hbm), (w0_ref, w1_ref, w2_ref), sems)

    def put(value, l, m):
        b = PAIR_AT[(l, m)]
        dv_ref[b * EPAD : (b + 1) * EPAD, :] = value.astype(BF16)

    for order, q_ref, w_ref in ((0, q0_ref, w0_ref), (1, q1_ref, w1_ref), (2, q2_ref, w2_ref)):
        copies[order].wait()
        blocks = 7 - order
        for k in range(0, blocks, 2):
            n = min(2, blocks - k)
            both = nt(q_ref[...], w_ref[k * C : (k + n) * C, :])
            for i in range(n):
                put(both[:EPAD, i * C : (i + 1) * C], order + k + i, order)
                if order > 0:
                    put(both[EPAD:, i * C : (i + 1) * C], order + k + i, -order)


def back_kernel(dv_ref, wt_ref, src_ref, own_ref, left_ref, mid_ref, right_ref,
                hot_ref, b_ref, sum_ref):
    one_hot_rows(slots_of(src_ref[...]), TAB, hot_ref)
    for l in range(LMAX + 1):
        rows = (2 * l + 1) * TAB
        for i, m in enumerate(KEPT[l]):
            fill_masked(wt_ref, hot_ref, l, m, b_ref, i * EPAD)
        n = len(KEPT[l])
        first = PAIR_AT[(l, KEPT[l][0])] * EPAD
        sum_ref[l * l * TAB : l * l * TAB + rows, :] = mm(
            b_ref[:rows, : n * EPAD], dv_ref[first : first + n * EPAD, :]
        )
    for j in range(ROWS):
        own_ref[j * OWN : (j + 1) * OWN, :] = sum_ref[j * TAB : j * TAB + OWN, :]
    outs = (left_ref, mid_ref, right_ref)
    for x in range(3):
        for y in range(3):
            for z in range(3):
                for a in range(2):
                    s = OWN + ((x * 3 + y) * 3 + z) * 2 + a
                    outs[x][y, z, a] = sum_ref[pl.ds(s, ROWS, stride=TAB), :].astype(BF16)


def v_kernel(coef_ref, left_ref, mid_ref, right_ref, wt_ref, src_ref, v0_ref, v1_ref, v2_ref,
             hot_ref, flat_ref, perm_ref, b_ref):
    one_hot_rows(slots_of(src_ref[...]), TAB, hot_ref)
    ins = (left_ref, mid_ref, right_ref)
    for x in range(3):
        for y in range(3):
            for z in range(3):
                for a in range(2):
                    s = ((x * 3 + y) * 3 + z) * 2 + a
                    flat_ref[s * PITCH : s * PITCH + ROWS, :] = ins[x][y, z, a].astype(F32)
    flat_ref[CELLS * PITCH :, :] = jnp.zeros(((TAB - OWN - CELLS) * PITCH, C), F32)
    for j in range(ROWS):
        perm_ref[j * TAB : j * TAB + OWN, :] = coef_ref[j * OWN : (j + 1) * OWN, :]
        perm_ref[j * TAB + OWN : (j + 1) * TAB, :] = flat_ref[
            pl.ds(j, TAB - OWN, stride=PITCH), :
        ].astype(BF16)
    tables = transposed_tables(perm_ref, TAB)
    outs = {0: v0_ref, 1: v1_ref, 2: v2_ref}
    for l in range(LMAX + 1):
        for m in KEPT[l]:
            fill_masked(wt_ref, hot_ref, l, m, b_ref, 0)
            v = mm(tables[l], b_ref[: (2 * l + 1) * TAB, :]).astype(BF16)
            k = (l - abs(m)) * C
            column = EPAD if m < 0 else 0
            outs[abs(m)][k : k + C, column : column + EPAD] = v


ORDER_ROWS = {0: 7, 1: 6, 2: 5}
PART_BLOCKS = (
    [(0, k) for k in range(7)] + [(1, k) for k in range(5)],
    [(1, k) for k in range(5, 12)] + [(2, k) for k in range(10)],
)
PART_ROWS = (80, 96)
LEAD = 8
TALL = 912


def grad_kernel(part, core_ref, *refs):
    orders = sorted({o for o, _ in PART_BLOCKS[part]})
    v_refs = dict(zip(orders, refs[: len(orders)]))
    q_refs = dict(zip(orders, refs[len(orders) : 2 * len(orders)]))
    keep_ref, send_ref, g_ref = refs[2 * len(orders) :]
    blocks = PART_BLOCKS[part]
    i = 0
    while i < len(blocks):
        order, k = blocks[i]
        n = 2 if i + 1 < len(blocks) and blocks[i + 1][0] == order else 1
        g = mm(v_refs[order][...], q_refs[order][:, k * C : (k + n) * C])
        rows = g.shape[0]
        for t in range(n):
            g_ref[i + t, LEAD : LEAD + rows, :] = g[:, t * C : (t + 1) * C]
        i += n
    source = []
    for i, (order, _) in enumerate(blocks):
        source += [(i, order, t) for t in range(ORDER_ROWS[order])]
    while len(source) < PART_ROWS[part]:
        i, order, t = source[-1]
        source.append((i, order, t + 1))
    place = lax.broadcasted_iota(jnp.int32, (8, C), 0)
    core = core_ref[0]

    def eight(p, first):
        value = None
        last = None
        for s in range(8):
            i, order, t = source[first + s]
            if i == last:
                continue
            last = i
            start = p * ORDER_ROWS[order] + (LEAD + t - s)
            rows = g_ref[i, pl.ds(start, 8), :]
            value = rows if value is None else jnp.where(place >= s, rows, value)
        return value

    def one(d, _):
        for h, out in ((0, keep_ref), (1, send_ref)):
            p = (d // 4) * 8 + (core ^ h) * 4 + d % 4
            for r in range(0, PART_ROWS[part], 16):
                out[d, r : r + 16, :] = jnp.concatenate(
                    [eight(p, r), eight(p, r + 8)], 0
                ).astype(BF16)
        return 0

    lax.fori_loop(0, 64, one, 0, unroll=2)


def u_kernel(v0_ref, v1_ref, v2_ref, ew_ref, tgt_ref, wt_ref, w0_hbm, w1_hbm, w2_hbm, out_ref,
             hot_ref, ewr_ref, v_ref, u_ref, a_ref, w0_ref, w1_ref, w2_ref, sems):
    copies = fetch((w0_hbm, w1_hbm, w2_hbm), (w0_ref, w1_ref, w2_ref), sems)
    one_hot_rows(tgt_ref[...], OWN, hot_ref)
    ewr_ref[...] = jnp.zeros(ewr_ref.shape, F32)
    ewr_ref[:, :EDGES] = jnp.broadcast_to(ew_ref[...], (C, EDGES))
    scale = ewr_ref[...].T
    unit = eye(EPAD, EPAD)

    def put(value, l, m):
        b = PAIR_AT[(l, m)]
        u_ref[b * EPAD : (b + 1) * EPAD, :] = (value * scale).astype(BF16)

    v_ref[:EPAD, :] = nt(unit, v0_ref[...]).astype(BF16)
    copies[0].wait()
    for k in range(0, 7, 2):
        n = min(2, 7 - k)
        u0 = mm(v_ref[:EPAD, :], w0_ref[:, k * C : (k + n) * C])
        for i in range(n):
            put(u0[:, i * C : (i + 1) * C], k + i, 0)
    for order, vt_ref, w_ref in ((1, v1_ref, w1_ref), (2, v2_ref, w2_ref)):
        n = vt_ref.shape[0]
        v_ref[:EPAD, :n] = nt(unit, vt_ref[:, :EPAD]).astype(BF16)
        v_ref[EPAD:, :n] = nt(unit, vt_ref[:, EPAD:]).astype(BF16)
        v = v_ref[:, :n]
        copies[order].wait()
        for k in range(0, 7 - order, 2):
            c = min(2, 7 - order - k)
            real = mm(v, w_ref[:, k * C : (k + c) * C])
            imag = mm(v, w_ref[:, n + k * C : n + (k + c) * C])
            plus = real[:EPAD] - imag[EPAD:]
            minus = real[EPAD:] + imag[:EPAD]
            for i in range(c):
                put(plus[:, i * C : (i + 1) * C], order + k + i, order)
                put(minus[:, i * C : (i + 1) * C], order + k + i, -order)
    for l in range(LMAX + 1):
        rows = (2 * l + 1) * OWN
        for i, m in enumerate(KEPT[l]):
            fill_masked(wt_ref, hot_ref, l, m, a_ref, i * EPAD)
        n = len(KEPT[l])
        first = PAIR_AT[(l, KEPT[l][0])] * EPAD
        out_ref[l * l * OWN : l * l * OWN + rows, :] = mm(
            a_ref[:rows, : n * EPAD], u_ref[first : first + n * EPAD, :]
        ).astype(BF16)


def total_kernel(in_ref, zero_ref, one_ref, two_ref, acc_ref):
    def add(d, total):
        return total + in_ref[d].astype(F32)

    acc_ref[...] = lax.fori_loop(1, 64, add, in_ref[0].astype(F32), unroll=7)
    for out, rows, blocks, runs in (
        (zero_ref, 7, 7, ((0, 7, 0),)),
        (one_ref, 6, 12, ((0, 5, 49), (5, 7, 80))),
        (two_ref, 5, 10, ((0, 10, 122),)),
    ):
        for t in range(rows):
            for first, count, offset in runs:
                out[t * blocks + first : t * blocks + first + count, :] = acc_ref[
                    pl.ds(offset + t, count, stride=rows), :
                ]


def owner_kernel(list_ref, own_ref, minus_ref, mid_ref, plus_ref, out_ref):
    out_ref[...] = own_ref[...]
    ins = (minus_ref, mid_ref, plus_ref)
    for x in range(3):
        for y in range(3):
            for z in range(3):
                cell = (x * 3 + y) * 3 + z
                if cell == 13:
                    continue
                k = cell if cell < 13 else cell - 1
                for a in range(2):
                    rows = pl.ds(list_ref[a, k], ROWS, stride=OWN)
                    out_ref[rows, :] = out_ref[rows, :] + ins[z][x, y, a].astype(F32)


def call(kernel, outs, scratch=(), scalars=0, inputs=0, far=0, flops=0, moved=0, vmem=16):
    specs = [pl.BlockSpec(memory_space=pltpu.SMEM)] * scalars
    specs += [pl.BlockSpec(memory_space=pltpu.VMEM)] * inputs
    specs += [pl.BlockSpec(memory_space=pl.ANY)] * far
    buffers = [pltpu.VMEM(s, d) for s, d in scratch]
    if far:
        buffers.append(pltpu.SemaphoreType.DMA((far,)))
    return pl.pallas_call(
        kernel,
        out_shape=[jax.ShapeDtypeStruct(s, d) for s, d in outs],
        in_specs=specs,
        out_specs=[pl.BlockSpec(memory_space=pltpu.VMEM)] * len(outs),
        scratch_shapes=buffers,
        compiler_params=pltpu.CompilerParams(vmem_limit_bytes=vmem * MIB),
        cost_estimate=pl.CostEstimate(flops=flops, bytes_accessed=moved, transcendentals=0),
    )


def shift(value, axis, step):
    count = lax.axis_size(axis)
    return lax.ppermute(value, axis, [(i, (i + step) % count) for i in range(count)])


AXES = ("gx", "gyx", "gyc", "gz")
GY = ("gyx", "gyc")
FACE = (3, 3, 2, ROWS, C)


def regroup(parts, index, axis):
    return jnp.stack([lax.index_in_dim(p, index, axis, keepdims=False) for p in parts], 1)


def by_component(atoms):
    return atoms.transpose(1, 0, 2).reshape(ROWS * OWN, C)


def by_atom(rows):
    return rows.reshape(ROWS, OWN, C).transpose(1, 0, 2)


WEIGHTS = [((896, 896), BF16), ((768, 1536), BF16), ((640, 1280), BF16)]
ORDERS = [((896, EPAD), BF16), ((768, 2 * EPAD), BF16), ((640, 2 * EPAD), BF16)]


def body(coefficients, send_list, sources, targets, wigner, edge_weight, cotangent, w_zero, w_one, w_two):
    listed = send_list.T
    src = sources.reshape(1, EDGES)
    tgt = targets.reshape(1, EDGES)
    ew = edge_weight.reshape(1, EDGES)
    core = lax.axis_index("gyc").astype(jnp.int32).reshape(1)
    coef = by_component(coefficients)

    z_minus, z_mid, z_plus = call(
        pick_kernel, [(FACE, BF16)] * 3, [((ROWS * OWN, C), F32)], scalars=1, inputs=1
    )(listed, coef)
    by_z = (shift(z_plus, "gz", 1), z_mid, shift(z_minus, "gz", -1))
    wt, q0, q1, q2 = call(
        q_kernel,
        [((456, EPAD), F32), ((EPAD, 896), BF16), ((512, 1536), BF16), ((512, 1280), BF16)],
        [((EPAD, 455), BF16), ((OWN, EPAD), BF16), ((8, EPAD), F32),
         ((13 * OWN, EPAD), BF16), ((3712, EPAD), BF16)],
        inputs=4, flops=2 * 10**9, moved=8 * 10**6,
    )(wigner, tgt, ew, by_component(cotangent))

    y_plus, y_minus = regroup(by_z, 2, 1), regroup(by_z, 0, 1)
    y_plus, y_minus, q0, q1, q2 = lax.optimization_barrier((y_plus, y_minus, q0, q1, q2))
    by_y = (shift(y_plus, GY, 1), regroup(by_z, 1, 1), shift(y_minus, GY, -1))
    (dv,) = call(
        dv_kernel, [((PAIRS * EPAD, C), BF16)], WEIGHTS, inputs=3, far=3,
        flops=3 * 10**9, moved=16 * 10**6, vmem=22,
    )(q0, q1, q2, w_zero, w_one, w_two)

    take_x = lambda i: jnp.stack([p[i] for p in by_y], 0)
    x_plus, x_minus, dv = lax.optimization_barrier((take_x(2), take_x(0), dv))
    left, mid, right = shift(x_plus, "gx", 1), take_x(1), shift(x_minus, "gx", -1)
    own, g_left, g_mid, g_right = call(
        back_kernel,
        [((ROWS * OWN, C), F32)] + [(FACE, BF16)] * 3,
        [((TAB, EPAD), BF16), ((13 * TAB, 5 * EPAD), BF16), ((ROWS * TAB, C), F32)],
        inputs=3, flops=3 * 10**9, moved=12 * 10**6,
    )(dv, wt, src)

    left, mid, right, g_left, g_right = lax.optimization_barrier((left, mid, right, g_left, g_right))
    by_x = (shift(g_right, "gx", 1), g_mid, shift(g_left, "gx", -1))
    v0, v1, v2 = call(
        v_kernel,
        ORDERS,
        [((TAB, EPAD), BF16), (((TAB - OWN) * PITCH, C), F32), ((ROWS * TAB, C), BF16),
         ((13 * TAB, EPAD), BF16)],
        inputs=6, flops=3 * 10**9, moved=8 * 10**6,
    )(coef, left, mid, right, wt, src)
    take_y = lambda i: jnp.stack([p[i] for p in by_x], 0)
    y_plus, y_minus, v0, v1, v2 = lax.optimization_barrier((take_y(2), take_y(0), v0, v1, v2))
    by_y = (shift(y_plus, GY, 1), take_y(1), shift(y_minus, GY, -1))

    def gradients(part, *operands):
        return call(
            functools.partial(grad_kernel, part),
            [((64, PART_ROWS[part], C), BF16)] * 2,
            [((len(PART_BLOCKS[part]), TALL, C), F32)],
            scalars=1, inputs=4, flops=2 * 10**9, moved=12 * 10**6, vmem=24,
        )(core, *operands)

    keep_a, send_a = gradients(0, v0, v1, q0, q1)
    take_z = lambda i: regroup(by_y, i, 1)
    z_plus, z_minus, keep_a, send_a, vb, vc = lax.optimization_barrier(
        (take_z(2), take_z(0), keep_a, send_a, v1, v2)
    )
    b_minus, b_mid, b_plus = shift(z_plus, "gz", 1), take_z(1), shift(z_minus, "gz", -1)
    received_a = shift(send_a, "gyc", 1)
    keep_b, send_b = gradients(1, vb, vc, q1, q2)
    received_b = shift(send_b, "gyc", 1)
    pair = jnp.concatenate(
        [
            (k.astype(F32) + r.astype(F32)).astype(BF16)
            for k, r in ((keep_a, received_a), (keep_b, received_b))
        ],
        1,
    )
    pair, b_minus, b_plus = lax.optimization_barrier((pair, b_minus, b_plus))
    pieces = lax.all_to_all(pair, ("gx", "gyx", "gz"), 0, 0, tiled=False)

    (updated,) = call(
        u_kernel,
        [((ROWS * OWN, C), BF16)],
        [((OWN, EPAD), BF16), ((C, EPAD), F32), ((2 * EPAD, 896), BF16),
         ((PAIRS * EPAD, C), BF16), ((13 * OWN, 5 * EPAD), BF16)] + WEIGHTS,
        inputs=6, far=3, flops=4 * 10**9, moved=20 * 10**6, vmem=24,
    )(v0, v1, v2, ew, tgt, wt, w_zero, w_one, w_two)
    (gradient,) = call(owner_kernel, [((ROWS * OWN, C), F32)], scalars=1, inputs=4)(
        listed, own, b_minus, b_mid, b_plus
    )
    zero, one, two = call(
        total_kernel,
        [((49, C), F32), ((72, C), F32), ((50, C), F32)],
        [((PIECE, C), F32)],
        inputs=1, flops=10**7, moved=4 * 10**6,
    )(pieces)
    return by_atom(updated), by_atom(gradient), zero.reshape(-1), one.reshape(-1), two.reshape(-1)


def solution(mesh):
    gx, gy, gz = mesh.devices.shape
    split = Mesh(mesh.devices.reshape(gx, gy // 2, 2, gz), AXES)
    lead = lambda rank: P(AXES, *([None] * (rank - 1)))
    in_specs = (lead(3), lead(2), lead(1), lead(1), lead(2), lead(1), lead(3), P(), P(), P())
    out_specs = (lead(3), lead(3), lead(1), lead(1), lead(1))
    return jax.shard_map(body, mesh=split, in_specs=in_specs, out_specs=out_specs, check_vma=False)
```

```python
import functools

import jax
import jax.numpy as jnp
from jax import lax
from jax.experimental import pallas as pl
from jax.experimental.pallas import tpu as pltpu
from jax.sharding import Mesh
from jax.sharding import PartitionSpec as P

F32 = jnp.float32
BF16 = jnp.bfloat16

LMAX = 6
ROWS = 49
C = 128
OWN = 16
CELLS = 54
TAB = 80
EDGES = 208
EPAD = 256
PITCH = 56
STARTS = [0, 1, 10, 35, 84, 165, 286, 455]

KEPT = [list(range(-min(l, 2), min(l, 2) + 1)) for l in range(LMAX + 1)]
PAIR_AT = {}
for _l in range(LMAX + 1):
    for _m in KEPT[_l]:
        PAIR_AT[(_l, _m)] = len(PAIR_AT)
PAIRS = len(PAIR_AT)
FIRST = {0: 0, 1: 7, -1: 13, 2: 19, -2: 24}


def order_block(l, m):
    return FIRST[m] + l - abs(m)


PIECE = 176
MIB = 1024 * 1024


def nt(left, right):
    return lax.dot_general(left, right, (((1,), (1,)), ((), ())), preferred_element_type=F32)


def mm(left, right):
    return jnp.dot(left, right, preferred_element_type=F32)


def eye(rows, columns, dtype=BF16):
    a = lax.broadcasted_iota(jnp.int32, (rows, columns), 0)
    b = lax.broadcasted_iota(jnp.int32, (rows, columns), 1)
    return (a == b).astype(F32).astype(dtype)


def one_hot_rows(index_row, rows, out_ref):
    a = lax.broadcasted_iota(jnp.int32, (rows, EDGES), 0)
    out_ref[...] = jnp.zeros(out_ref.shape, out_ref.dtype)
    out_ref[:, :EDGES] = (a == index_row).astype(F32).astype(BF16)


def slots_of(sources_row):
    return sources_row + jnp.where(sources_row >= OWN + 26, 2, 0)


def fill_masked(wt_ref, hot_ref, l, m, out_ref, column):
    rows = hot_ref.shape[0]
    width = 2 * l + 1
    for j in range(width):
        at = STARTS[l] + (l + m) * width + j
        row = jnp.broadcast_to(wt_ref[at : at + 1, :], (16, EPAD)).astype(BF16)
        for g in range(0, rows, 16):
            out_ref[j * rows + g : j * rows + g + 16, column : column + EPAD] = (
                hot_ref[g : g + 16, :] * row
            )


def transposed_tables(perm_ref, slots):
    unit = eye(C, C)
    return [
        nt(unit, perm_ref[l * l * slots : (l + 1) * (l + 1) * slots, :]).astype(BF16)
        for l in range(LMAX + 1)
    ]


def pick_kernel(list_ref, coef_ref, minus_ref, mid_ref, plus_ref, flat_ref):
    flat_ref[...] = coef_ref[...].astype(F32)
    outs = (minus_ref, mid_ref, plus_ref)
    for x in range(3):
        for y in range(3):
            for z in range(3):
                cell = (x * 3 + y) * 3 + z
                for a in range(2):
                    if cell == 13:
                        outs[z][x, y, a] = jnp.zeros((ROWS, C), BF16)
                    else:
                        k = cell if cell < 13 else cell - 1
                        outs[z][x, y, a] = flat_ref[
                            pl.ds(list_ref[a, k], ROWS, stride=OWN), :
                        ].astype(BF16)


def q_kernel(wig_ref, tgt_ref, ew_ref, cot_ref, wt_ref, q0_ref, q1_ref, q2_ref,
             pad_ref, hot_ref, ewr_ref, a_ref, qt_ref):
    pad_ref[...] = jnp.zeros(pad_ref.shape, BF16)
    pad_ref[:EDGES, :] = wig_ref[...]
    wt_ref[...] = nt(eye(456, 455), pad_ref[...])
    one_hot_rows(tgt_ref[...], OWN, hot_ref)
    ewr_ref[...] = jnp.zeros(ewr_ref.shape, F32)
    ewr_ref[:, :EDGES] = jnp.broadcast_to(ew_ref[...], (8, EDGES))
    tables = transposed_tables(cot_ref, OWN)
    scale = ewr_ref[0:1, :]
    for l in range(LMAX + 1):
        for m in KEPT[l]:
            fill_masked(wt_ref, hot_ref, l, m, a_ref, 0)
            q = mm(tables[l], a_ref[: (2 * l + 1) * OWN, :]) * scale
            b = order_block(l, m)
            qt_ref[b * C : (b + 1) * C, :] = q.astype(BF16)
    unit = eye(EPAD, EPAD)
    q0_ref[...] = nt(unit, qt_ref[0:896, :]).astype(BF16)
    for out, start, n in ((q1_ref, 896, 768), (q2_ref, 2432, 640)):
        plus = nt(unit, qt_ref[start : start + n, :]).astype(BF16)
        minus = nt(unit, qt_ref[start + n : start + 2 * n, :]).astype(BF16)
        out[0:EPAD, 0:n] = plus
        out[0:EPAD, n : 2 * n] = minus
        out[EPAD : 2 * EPAD, 0:n] = minus
        out[EPAD : 2 * EPAD, n : 2 * n] = -plus


def dv_kernel(q0_ref, q1_ref, q2_ref, w0_ref, w1_ref, w2_ref, dv_ref):
    def put(value, l, m):
        b = PAIR_AT[(l, m)]
        dv_ref[b * EPAD : (b + 1) * EPAD, :] = value.astype(BF16)

    for order, q_ref, w_ref in ((0, q0_ref, w0_ref), (1, q1_ref, w1_ref), (2, q2_ref, w2_ref)):
        blocks = 7 - order
        for k in range(0, blocks, 2):
            n = min(2, blocks - k)
            both = nt(q_ref[...], w_ref[k * C : (k + n) * C, :])
            for i in range(n):
                put(both[:EPAD, i * C : (i + 1) * C], order + k + i, order)
                if order > 0:
                    put(both[EPAD:, i * C : (i + 1) * C], order + k + i, -order)


def back_kernel(dv_ref, wt_ref, src_ref, own_ref, minus_ref, mid_ref, plus_ref,
                hot_ref, b_ref, sum_ref):
    one_hot_rows(slots_of(src_ref[...]), TAB, hot_ref)
    for l in range(LMAX + 1):
        rows = (2 * l + 1) * TAB
        for i, m in enumerate(KEPT[l]):
            fill_masked(wt_ref, hot_ref, l, m, b_ref, i * EPAD)
        n = len(KEPT[l])
        first = PAIR_AT[(l, KEPT[l][0])] * EPAD
        sum_ref[l * l * TAB : l * l * TAB + rows, :] = mm(
            b_ref[:rows, : n * EPAD], dv_ref[first : first + n * EPAD, :]
        )
    for j in range(ROWS):
        own_ref[j * OWN : (j + 1) * OWN, :] = sum_ref[j * TAB : j * TAB + OWN, :]
    outs = (minus_ref, mid_ref, plus_ref)
    for x in range(3):
        for y in range(3):
            for z in range(3):
                for a in range(2):
                    s = OWN + ((x * 3 + y) * 3 + z) * 2 + a
                    outs[z][x, y, a] = sum_ref[pl.ds(s, ROWS, stride=TAB), :].astype(BF16)


def v_kernel(coef_ref, left_ref, mid_ref, right_ref, wt_ref, src_ref, v0_ref, v1_ref, v2_ref,
             hot_ref, flat_ref, perm_ref, b_ref):
    one_hot_rows(slots_of(src_ref[...]), TAB, hot_ref)
    ins = (left_ref, mid_ref, right_ref)
    for x in range(3):
        for y in range(3):
            for z in range(3):
                for a in range(2):
                    s = ((x * 3 + y) * 3 + z) * 2 + a
                    flat_ref[s * PITCH : s * PITCH + ROWS, :] = ins[x][y, z, a].astype(F32)
    flat_ref[CELLS * PITCH :, :] = jnp.zeros(((TAB - OWN - CELLS) * PITCH, C), F32)
    for j in range(ROWS):
        perm_ref[j * TAB : j * TAB + OWN, :] = coef_ref[j * OWN : (j + 1) * OWN, :]
        perm_ref[j * TAB + OWN : (j + 1) * TAB, :] = flat_ref[
            pl.ds(j, TAB - OWN, stride=PITCH), :
        ].astype(BF16)
    tables = transposed_tables(perm_ref, TAB)
    outs = {0: v0_ref, 1: v1_ref, 2: v2_ref}
    for l in range(LMAX + 1):
        for m in KEPT[l]:
            fill_masked(wt_ref, hot_ref, l, m, b_ref, 0)
            v = mm(tables[l], b_ref[: (2 * l + 1) * TAB, :]).astype(BF16)
            k = (l - abs(m)) * C
            column = EPAD if m < 0 else 0
            outs[abs(m)][k : k + C, column : column + EPAD] = v


ORDER_ROWS = {0: 7, 1: 6, 2: 5}
BLOCKS = [(0, k) for k in range(7)] + [(1, k) for k in range(12)] + [(2, k) for k in range(10)]
LEAD = 8
TALL = 912


def grad_kernel(core_ref, v0_ref, v1_ref, v2_ref, q0_ref, q1_ref, q2_ref, keep_ref, send_ref, g_ref):
    v_refs = (v0_ref, v1_ref, v2_ref)
    q_refs = (q0_ref, q1_ref, q2_ref)
    blocks = BLOCKS
    i = 0
    while i < len(blocks):
        order, k = blocks[i]
        n = 2 if i + 1 < len(blocks) and blocks[i + 1][0] == order else 1
        g = mm(v_refs[order][...], q_refs[order][:, k * C : (k + n) * C])
        rows = g.shape[0]
        for t in range(n):
            g_ref[i + t, LEAD : LEAD + rows, :] = g[:, t * C : (t + 1) * C]
        i += n
    source = []
    for i, (order, _) in enumerate(blocks):
        source += [(i, order, t) for t in range(ORDER_ROWS[order])]
    while len(source) < PIECE:
        i, order, t = source[-1]
        source.append((i, order, t + 1))
    place = lax.broadcasted_iota(jnp.int32, (8, C), 0)
    core = core_ref[0]

    def eight(p, first):
        value = None
        last = None
        for s in range(8):
            i, order, t = source[first + s]
            if i == last:
                continue
            last = i
            start = p * ORDER_ROWS[order] + (LEAD + t - s)
            rows = g_ref[i, pl.ds(start, 8), :]
            value = rows if value is None else jnp.where(place >= s, rows, value)
        return value

    def one(d, _):
        for h, out in ((0, keep_ref), (1, send_ref)):
            p = (d // 4) * 8 + (core ^ h) * 4 + d % 4
            for r in range(0, PIECE, 16):
                out[d, r : r + 16, :] = jnp.concatenate(
                    [eight(p, r), eight(p, r + 8)], 0
                ).astype(BF16)
        return 0

    lax.fori_loop(0, 64, one, 0, unroll=2)


def u_kernel(v0_ref, v1_ref, v2_ref, ew_ref, tgt_ref, wt_ref, w0_ref, w1_ref, w2_ref, out_ref,
             hot_ref, ewr_ref, v_ref, u_ref, a_ref):
    one_hot_rows(tgt_ref[...], OWN, hot_ref)
    ewr_ref[...] = jnp.zeros(ewr_ref.shape, F32)
    ewr_ref[:, :EDGES] = jnp.broadcast_to(ew_ref[...], (C, EDGES))
    scale = ewr_ref[...].T
    unit = eye(EPAD, EPAD)

    def put(value, l, m):
        b = PAIR_AT[(l, m)]
        u_ref[b * EPAD : (b + 1) * EPAD, :] = (value * scale).astype(BF16)

    v_ref[:EPAD, :] = nt(unit, v0_ref[...]).astype(BF16)
    for k in range(0, 7, 2):
        n = min(2, 7 - k)
        u0 = mm(v_ref[:EPAD, :], w0_ref[:, k * C : (k + n) * C])
        for i in range(n):
            put(u0[:, i * C : (i + 1) * C], k + i, 0)
    for order, vt_ref, w_ref in ((1, v1_ref, w1_ref), (2, v2_ref, w2_ref)):
        n = vt_ref.shape[0]
        v_ref[:EPAD, :n] = nt(unit, vt_ref[:, :EPAD]).astype(BF16)
        v_ref[EPAD:, :n] = nt(unit, vt_ref[:, EPAD:]).astype(BF16)
        v = v_ref[:, :n]
        for k in range(0, 7 - order, 2):
            c = min(2, 7 - order - k)
            real = mm(v, w_ref[:, k * C : (k + c) * C])
            imag = mm(v, w_ref[:, n + k * C : n + (k + c) * C])
            plus = real[:EPAD] - imag[EPAD:]
            minus = real[EPAD:] + imag[:EPAD]
            for i in range(c):
                put(plus[:, i * C : (i + 1) * C], order + k + i, order)
                put(minus[:, i * C : (i + 1) * C], order + k + i, -order)
    for l in range(LMAX + 1):
        rows = (2 * l + 1) * OWN
        for i, m in enumerate(KEPT[l]):
            fill_masked(wt_ref, hot_ref, l, m, a_ref, i * EPAD)
        n = len(KEPT[l])
        first = PAIR_AT[(l, KEPT[l][0])] * EPAD
        out_ref[l * l * OWN : l * l * OWN + rows, :] = mm(
            a_ref[:rows, : n * EPAD], u_ref[first : first + n * EPAD, :]
        ).astype(BF16)


def total_kernel(in_ref, zero_ref, one_ref, two_ref, acc_ref):
    def add(d, total):
        return total + in_ref[d].astype(F32)

    acc_ref[...] = lax.fori_loop(1, 64, add, in_ref[0].astype(F32), unroll=7)
    for out, rows, blocks, runs in (
        (zero_ref, 7, 7, ((0, 7, 0),)),
        (one_ref, 6, 12, ((0, 12, 49),)),
        (two_ref, 5, 10, ((0, 10, 121),)),
    ):
        for t in range(rows):
            for first, count, offset in runs:
                out[t * blocks + first : t * blocks + first + count, :] = acc_ref[
                    pl.ds(offset + t, count, stride=rows), :
                ]


def owner_kernel(list_ref, own_ref, minus_ref, left_ref, mid_ref, right_ref, plus_ref, out_ref):
    out_ref[...] = own_ref[...]
    middle = (left_ref, mid_ref, right_ref)
    for x in range(3):
        for y in range(3):
            for z in range(3):
                cell = (x * 3 + y) * 3 + z
                if cell == 13:
                    continue
                face = middle[x].at[z, 1] if y == 1 else (minus_ref if y == 0 else plus_ref).at[z, x]
                k = cell if cell < 13 else cell - 1
                for a in range(2):
                    rows = pl.ds(list_ref[a, k], ROWS, stride=OWN)
                    out_ref[rows, :] = out_ref[rows, :] + face[a].astype(F32)


def pair_kernel(keep_ref, received_ref, out_ref):
    def one(d, _):
        out_ref[d] = keep_ref[d] + received_ref[d]
        return 0

    lax.fori_loop(0, 64, one, 0, unroll=4)


def call(kernel, outs, scratch=(), scalars=0, inputs=0, flops=0, moved=0, vmem=16):
    specs = [pl.BlockSpec(memory_space=pltpu.SMEM)] * scalars
    specs += [pl.BlockSpec(memory_space=pltpu.VMEM)] * inputs
    return pl.pallas_call(
        kernel,
        out_shape=[jax.ShapeDtypeStruct(s, d) for s, d in outs],
        in_specs=specs,
        out_specs=[pl.BlockSpec(memory_space=pltpu.VMEM)] * len(outs),
        scratch_shapes=[pltpu.VMEM(s, d) for s, d in scratch],
        compiler_params=pltpu.CompilerParams(vmem_limit_bytes=vmem * MIB),
        cost_estimate=pl.CostEstimate(flops=flops, bytes_accessed=moved, transcendentals=0),
    )


def shift(value, axis, step):
    count = lax.axis_size(axis)
    return lax.ppermute(value, axis, [(i, (i + step) % count) for i in range(count)])


AXES = ("gx", "gyx", "gyc", "gz")
GY = ("gyx", "gyc")
FACE = (3, 3, 2, ROWS, C)


def regroup(parts, index, axis):
    return jnp.stack([lax.index_in_dim(p, index, axis, keepdims=False) for p in parts], 1)


def by_component(atoms):
    return atoms.transpose(1, 0, 2).reshape(ROWS * OWN, C)


def by_atom(rows):
    return rows.reshape(ROWS, OWN, C).transpose(1, 0, 2)


ORDERS = [((896, EPAD), BF16), ((768, 2 * EPAD), BF16), ((640, 2 * EPAD), BF16)]


def body(coefficients, send_list, sources, targets, wigner, edge_weight, cotangent, w_zero, w_one, w_two):
    listed = send_list.T
    src = sources.reshape(1, EDGES)
    tgt = targets.reshape(1, EDGES)
    ew = edge_weight.reshape(1, EDGES)
    core = lax.axis_index("gyc").astype(jnp.int32).reshape(1)
    coef = by_component(coefficients)

    z_minus, z_mid, z_plus = call(
        pick_kernel, [(FACE, BF16)] * 3, [((ROWS * OWN, C), F32)], scalars=1, inputs=1
    )(listed, coef)
    by_z = (shift(z_plus, "gz", 1), z_mid, shift(z_minus, "gz", -1))
    wt, q0, q1, q2 = call(
        q_kernel,
        [((456, EPAD), F32), ((EPAD, 896), BF16), ((512, 1536), BF16), ((512, 1280), BF16)],
        [((EPAD, 455), BF16), ((OWN, EPAD), BF16), ((8, EPAD), F32),
         ((13 * OWN, EPAD), BF16), ((3712, EPAD), BF16)],
        inputs=4, flops=2 * 10**9, moved=8 * 10**6,
    )(wigner, tgt, ew, by_component(cotangent))

    first, last, q0, q1, q2 = lax.optimization_barrier((by_z[0], by_z[2], q0, q1, q2))
    by_z = (first, z_mid, last)
    by_y = (
        shift(regroup(by_z, 2, 1), GY, 1), regroup(by_z, 1, 1), shift(regroup(by_z, 0, 1), GY, -1)
    )
    (dv,) = call(
        dv_kernel, [((PAIRS * EPAD, C), BF16)], inputs=6,
        flops=3 * 10**9, moved=16 * 10**6,
    )(q0, q1, q2, w_zero, w_one, w_two)

    own, g_minus, g_mid, g_plus = call(
        back_kernel,
        [((ROWS * OWN, C), F32)] + [(FACE, BF16)] * 3,
        [((TAB, EPAD), BF16), ((13 * TAB, 5 * EPAD), BF16), ((ROWS * TAB, C), F32)],
        inputs=3, flops=3 * 10**9, moved=12 * 10**6,
    )(dv, wt, src)
    first, last, g_minus, g_plus = lax.optimization_barrier((by_y[0], by_y[2], g_minus, g_plus))
    by_y = (first, by_y[1], last)
    take_x = lambda i: jnp.stack([p[i] for p in by_y], 0)
    left, mid, right = shift(take_x(2), "gx", 1), take_x(1), shift(take_x(0), "gx", -1)

    by_z = (shift(g_plus, "gz", 1), g_mid, shift(g_minus, "gz", -1))
    v0, v1, v2 = call(
        v_kernel,
        ORDERS,
        [((TAB, EPAD), BF16), (((TAB - OWN) * PITCH, C), F32), ((ROWS * TAB, C), BF16),
         ((13 * TAB, EPAD), BF16)],
        inputs=6, flops=3 * 10**9, moved=8 * 10**6,
    )(coef, left, mid, right, wt, src)

    first, last, v0, v1, v2 = lax.optimization_barrier((by_z[0], by_z[2], v0, v1, v2))
    by_z = (first, g_mid, last)
    back_x = lambda x: jnp.stack([p[x] for p in by_z], 0)
    by_x = (shift(back_x(2), "gx", 1), back_x(1), shift(back_x(0), "gx", -1))
    keep, send = call(
        grad_kernel,
        [((64, PIECE, C), BF16)] * 2,
        [((len(BLOCKS), TALL, C), F32)],
        scalars=1, inputs=6, flops=4 * 10**9, moved=24 * 10**6, vmem=30,
    )(core, v0, v1, v2, q0, q1, q2)
    first, last, keep, send = lax.optimization_barrier((by_x[0], by_x[2], keep, send))
    by_x = (first, by_x[1], last)
    received = shift(send, "gyc", 1)
    back_y = lambda y: regroup(by_x, y, 1)
    b_minus, b_plus = shift(back_y(2), GY, 1), shift(back_y(0), GY, -1)
    (pair,) = call(pair_kernel, [((64, PIECE, C), BF16)], inputs=2, flops=10**7, moved=10**7)(
        keep, received
    )
    pair, b_minus, b_plus = lax.optimization_barrier((pair, b_minus, b_plus))
    pieces = lax.all_to_all(pair, ("gx", "gyx", "gz"), 0, 0, tiled=False)

    (updated,) = call(
        u_kernel,
        [((ROWS * OWN, C), BF16)],
        [((OWN, EPAD), BF16), ((C, EPAD), F32), ((2 * EPAD, 896), BF16),
         ((PAIRS * EPAD, C), BF16), ((13 * OWN, 5 * EPAD), BF16)],
        inputs=9, flops=4 * 10**9, moved=20 * 10**6,
    )(v0, v1, v2, ew, tgt, wt, w_zero, w_one, w_two)
    (gradient,) = call(owner_kernel, [((ROWS * OWN, C), F32)], scalars=1, inputs=6)(
        listed, own, b_minus, *by_x, b_plus
    )
    zero, one, two = call(
        total_kernel,
        [((49, C), F32), ((72, C), F32), ((50, C), F32)],
        [((PIECE, C), F32)],
        inputs=1, flops=10**7, moved=4 * 10**6,
    )(pieces)
    return by_atom(updated), by_atom(gradient), zero.reshape(-1), one.reshape(-1), two.reshape(-1)


def solution(mesh):
    gx, gy, gz = mesh.devices.shape
    split = Mesh(mesh.devices.reshape(gx, gy // 2, 2, gz), AXES)
    lead = lambda rank: P(AXES, *([None] * (rank - 1)))
    in_specs = (lead(3), lead(2), lead(1), lead(1), lead(2), lead(1), lead(3), P(), P(), P())
    out_specs = (lead(3), lead(3), lead(1), lead(1), lead(1))
    return jax.shard_map(body, mesh=split, in_specs=in_specs, out_specs=out_specs, check_vma=False)
```

```python
import functools

import jax
import jax.numpy as jnp
from jax import lax
from jax.experimental import pallas as pl
from jax.experimental.pallas import tpu as pltpu
from jax.sharding import Mesh
from jax.sharding import PartitionSpec as P

F32 = jnp.float32
BF16 = jnp.bfloat16

LMAX = 6
ROWS = 49
C = 128
OWN = 16
CELLS = 54
TAB = 80
EDGES = 208
EPAD = 256
PITCH = 56
STARTS = [0, 1, 10, 35, 84, 165, 286, 455]

KEPT = [list(range(-min(l, 2), min(l, 2) + 1)) for l in range(LMAX + 1)]
PAIR_AT = {}
for _l in range(LMAX + 1):
    for _m in KEPT[_l]:
        PAIR_AT[(_l, _m)] = len(PAIR_AT)
PAIRS = len(PAIR_AT)
FIRST = {0: 0, 1: 7, -1: 13, 2: 19, -2: 24}


def order_block(l, m):
    return FIRST[m] + l - abs(m)


PIECE = 176
MIB = 1024 * 1024


def nt(left, right):
    return lax.dot_general(left, right, (((1,), (1,)), ((), ())), preferred_element_type=F32)


def mm(left, right):
    return jnp.dot(left, right, preferred_element_type=F32)


def eye(rows, columns, dtype=BF16):
    a = lax.broadcasted_iota(jnp.int32, (rows, columns), 0)
    b = lax.broadcasted_iota(jnp.int32, (rows, columns), 1)
    return (a == b).astype(F32).astype(dtype)


def one_hot_rows(index_row, rows, out_ref):
    a = lax.broadcasted_iota(jnp.int32, (rows, EDGES), 0)
    out_ref[...] = jnp.zeros(out_ref.shape, out_ref.dtype)
    out_ref[:, :EDGES] = (a == index_row).astype(F32).astype(BF16)


def slots_of(sources_row):
    return sources_row + jnp.where(sources_row >= OWN + 26, 2, 0)


def fill_masked(wt_ref, hot_ref, l, m, out_ref, column):
    rows = hot_ref.shape[0]
    width = 2 * l + 1
    for j in range(width):
        at = STARTS[l] + (l + m) * width + j
        row = jnp.broadcast_to(wt_ref[at : at + 1, :], (16, EPAD)).astype(BF16)
        for g in range(0, rows, 16):
            out_ref[j * rows + g : j * rows + g + 16, column : column + EPAD] = (
                hot_ref[g : g + 16, :] * row
            )


def transposed_tables(perm_ref, slots):
    unit = eye(C, C)
    return [
        nt(unit, perm_ref[l * l * slots : (l + 1) * (l + 1) * slots, :]).astype(BF16)
        for l in range(LMAX + 1)
    ]


def pick_kernel(list_ref, coef_ref, minus_ref, mid_ref, plus_ref, flat_ref):
    flat_ref[...] = coef_ref[...].astype(F32)
    outs = (minus_ref, mid_ref, plus_ref)
    for x in range(3):
        for y in range(3):
            for z in range(3):
                cell = (x * 3 + y) * 3 + z
                for a in range(2):
                    if cell == 13:
                        outs[z][x, y, a] = jnp.zeros((ROWS, C), BF16)
                    else:
                        k = cell if cell < 13 else cell - 1
                        outs[z][x, y, a] = flat_ref[
                            pl.ds(list_ref[a, k], ROWS, stride=OWN), :
                        ].astype(BF16)


def q_kernel(wig_ref, tgt_ref, ew_ref, cot_ref, wt_ref, q0_ref, q1_ref, q2_ref,
             pad_ref, hot_ref, ewr_ref, a_ref, qt_ref):
    pad_ref[...] = jnp.zeros(pad_ref.shape, BF16)
    pad_ref[:EDGES, :] = wig_ref[...]
    wt_ref[...] = nt(eye(456, 455), pad_ref[...])
    one_hot_rows(tgt_ref[...], OWN, hot_ref)
    ewr_ref[...] = jnp.zeros(ewr_ref.shape, F32)
    ewr_ref[:, :EDGES] = jnp.broadcast_to(ew_ref[...], (8, EDGES))
    tables = transposed_tables(cot_ref, OWN)
    scale = ewr_ref[0:1, :]
    for l in range(LMAX + 1):
        for m in KEPT[l]:
            fill_masked(wt_ref, hot_ref, l, m, a_ref, 0)
            q = mm(tables[l], a_ref[: (2 * l + 1) * OWN, :]) * scale
            b = order_block(l, m)
            qt_ref[b * C : (b + 1) * C, :] = q.astype(BF16)
    unit = eye(EPAD, EPAD)
    q0_ref[...] = nt(unit, qt_ref[0:896, :]).astype(BF16)
    for out, start, n in ((q1_ref, 896, 768), (q2_ref, 2432, 640)):
        plus = nt(unit, qt_ref[start : start + n, :]).astype(BF16)
        minus = nt(unit, qt_ref[start + n : start + 2 * n, :]).astype(BF16)
        out[0:EPAD, 0:n] = plus
        out[0:EPAD, n : 2 * n] = minus
        out[EPAD : 2 * EPAD, 0:n] = minus
        out[EPAD : 2 * EPAD, n : 2 * n] = -plus


def dv_kernel(q0_ref, q1_ref, q2_ref, w0_ref, w1_ref, w2_ref, dv_ref):
    def put(value, l, m):
        b = PAIR_AT[(l, m)]
        dv_ref[b * EPAD : (b + 1) * EPAD, :] = value.astype(BF16)

    for order, q_ref, w_ref in ((0, q0_ref, w0_ref), (1, q1_ref, w1_ref), (2, q2_ref, w2_ref)):
        blocks = 7 - order
        for k in range(0, blocks, 2):
            n = min(2, blocks - k)
            both = nt(q_ref[...], w_ref[k * C : (k + n) * C, :])
            for i in range(n):
                put(both[:EPAD, i * C : (i + 1) * C], order + k + i, order)
                if order > 0:
                    put(both[EPAD:, i * C : (i + 1) * C], order + k + i, -order)


def back_kernel(dv_ref, wt_ref, src_ref, own_ref, minus_ref, mid_ref, plus_ref,
                hot_ref, b_ref, sum_ref):
    one_hot_rows(slots_of(src_ref[...]), TAB, hot_ref)
    for l in range(LMAX + 1):
        rows = (2 * l + 1) * TAB
        for i, m in enumerate(KEPT[l]):
            fill_masked(wt_ref, hot_ref, l, m, b_ref, i * EPAD)
        n = len(KEPT[l])
        first = PAIR_AT[(l, KEPT[l][0])] * EPAD
        sum_ref[l * l * TAB : l * l * TAB + rows, :] = mm(
            b_ref[:rows, : n * EPAD], dv_ref[first : first + n * EPAD, :]
        )
    for j in range(ROWS):
        own_ref[j * OWN : (j + 1) * OWN, :] = sum_ref[j * TAB : j * TAB + OWN, :]
    outs = (minus_ref, mid_ref, plus_ref)
    for x in range(3):
        for y in range(3):
            for z in range(3):
                for a in range(2):
                    s = OWN + ((x * 3 + y) * 3 + z) * 2 + a
                    outs[z][x, y, a] = sum_ref[pl.ds(s, ROWS, stride=TAB), :].astype(BF16)


def v_kernel(coef_ref, left_ref, mid_ref, right_ref, wt_ref, src_ref, v0_ref, v1_ref, v2_ref,
             hot_ref, flat_ref, perm_ref, b_ref):
    one_hot_rows(slots_of(src_ref[...]), TAB, hot_ref)
    ins = (left_ref, mid_ref, right_ref)
    for x in range(3):
        for y in range(3):
            for z in range(3):
                for a in range(2):
                    s = ((x * 3 + y) * 3 + z) * 2 + a
                    flat_ref[s * PITCH : s * PITCH + ROWS, :] = ins[x][y, z, a].astype(F32)
    flat_ref[CELLS * PITCH :, :] = jnp.zeros(((TAB - OWN - CELLS) * PITCH, C), F32)
    for j in range(ROWS):
        perm_ref[j * TAB : j * TAB + OWN, :] = coef_ref[j * OWN : (j + 1) * OWN, :]
        perm_ref[j * TAB + OWN : (j + 1) * TAB, :] = flat_ref[
            pl.ds(j, TAB - OWN, stride=PITCH), :
        ].astype(BF16)
    tables = transposed_tables(perm_ref, TAB)
    outs = {0: v0_ref, 1: v1_ref, 2: v2_ref}
    for l in range(LMAX + 1):
        for m in KEPT[l]:
            fill_masked(wt_ref, hot_ref, l, m, b_ref, 0)
            v = mm(tables[l], b_ref[: (2 * l + 1) * TAB, :]).astype(BF16)
            k = (l - abs(m)) * C
            column = EPAD if m < 0 else 0
            outs[abs(m)][k : k + C, column : column + EPAD] = v


ORDER_ROWS = {0: 7, 1: 6, 2: 5}
BLOCKS = [(0, k) for k in range(7)] + [(1, k) for k in range(12)] + [(2, k) for k in range(10)]
LEAD = 8
TALL = 912


def grad_kernel(core_ref, v0_ref, v1_ref, v2_ref, q0_ref, q1_ref, q2_ref, keep_ref, send_ref, g_ref):
    v_refs = (v0_ref, v1_ref, v2_ref)
    q_refs = (q0_ref, q1_ref, q2_ref)
    blocks = BLOCKS
    i = 0
    while i < len(blocks):
        order, k = blocks[i]
        n = 2 if i + 1 < len(blocks) and blocks[i + 1][0] == order else 1
        g = mm(v_refs[order][...], q_refs[order][:, k * C : (k + n) * C])
        rows = g.shape[0]
        for t in range(n):
            g_ref[i + t, LEAD : LEAD + rows, :] = g[:, t * C : (t + 1) * C]
        i += n
    source = []
    for i, (order, _) in enumerate(blocks):
        source += [(i, order, t) for t in range(ORDER_ROWS[order])]
    while len(source) < PIECE:
        i, order, t = source[-1]
        source.append((i, order, t + 1))
    place = lax.broadcasted_iota(jnp.int32, (8, C), 0)
    core = core_ref[0]

    def eight(p, first):
        value = None
        last = None
        for s in range(8):
            i, order, t = source[first + s]
            if i == last:
                continue
            last = i
            start = p * ORDER_ROWS[order] + (LEAD + t - s)
            rows = g_ref[i, pl.ds(start, 8), :]
            value = rows if value is None else jnp.where(place >= s, rows, value)
        return value

    def one(d, _):
        for h, out in ((0, keep_ref), (1, send_ref)):
            p = (d // 4) * 8 + (core ^ h) * 4 + d % 4
            for r in range(0, PIECE, 16):
                out[d, r : r + 16, :] = jnp.concatenate(
                    [eight(p, r), eight(p, r + 8)], 0
                ).astype(BF16)
        return 0

    lax.fori_loop(0, 64, one, 0, unroll=2)


def u_kernel(v0_ref, v1_ref, v2_ref, ew_ref, tgt_ref, wt_ref, w0_ref, w1_ref, w2_ref, out_ref,
             hot_ref, ewr_ref, v_ref, u_ref, a_ref):
    one_hot_rows(tgt_ref[...], OWN, hot_ref)
    ewr_ref[...] = jnp.zeros(ewr_ref.shape, F32)
    ewr_ref[:, :EDGES] = jnp.broadcast_to(ew_ref[...], (C, EDGES))
    scale = ewr_ref[...].T
    unit = eye(EPAD, EPAD)

    def put(value, l, m):
        b = PAIR_AT[(l, m)]
        u_ref[b * EPAD : (b + 1) * EPAD, :] = (value * scale).astype(BF16)

    v_ref[:EPAD, :] = nt(unit, v0_ref[...]).astype(BF16)
    for k in range(0, 7, 2):
        n = min(2, 7 - k)
        u0 = mm(v_ref[:EPAD, :], w0_ref[:, k * C : (k + n) * C])
        for i in range(n):
            put(u0[:, i * C : (i + 1) * C], k + i, 0)
    for order, vt_ref, w_ref in ((1, v1_ref, w1_ref), (2, v2_ref, w2_ref)):
        n = vt_ref.shape[0]
        v_ref[:EPAD, :n] = nt(unit, vt_ref[:, :EPAD]).astype(BF16)
        v_ref[EPAD:, :n] = nt(unit, vt_ref[:, EPAD:]).astype(BF16)
        v = v_ref[:, :n]
        for k in range(0, 7 - order, 2):
            c = min(2, 7 - order - k)
            real = mm(v, w_ref[:, k * C : (k + c) * C])
            imag = mm(v, w_ref[:, n + k * C : n + (k + c) * C])
            plus = real[:EPAD] - imag[EPAD:]
            minus = real[EPAD:] + imag[:EPAD]
            for i in range(c):
                put(plus[:, i * C : (i + 1) * C], order + k + i, order)
                put(minus[:, i * C : (i + 1) * C], order + k + i, -order)
    for l in range(LMAX + 1):
        rows = (2 * l + 1) * OWN
        for i, m in enumerate(KEPT[l]):
            fill_masked(wt_ref, hot_ref, l, m, a_ref, i * EPAD)
        n = len(KEPT[l])
        first = PAIR_AT[(l, KEPT[l][0])] * EPAD
        out_ref[l * l * OWN : l * l * OWN + rows, :] = mm(
            a_ref[:rows, : n * EPAD], u_ref[first : first + n * EPAD, :]
        ).astype(BF16)


def total_kernel(in_ref, zero_ref, one_ref, two_ref, acc_ref):
    def add(d, total):
        return total + in_ref[d].astype(F32)

    acc_ref[...] = lax.fori_loop(1, 64, add, in_ref[0].astype(F32), unroll=7)
    for out, rows, blocks, runs in (
        (zero_ref, 7, 7, ((0, 7, 0),)),
        (one_ref, 6, 12, ((0, 12, 49),)),
        (two_ref, 5, 10, ((0, 10, 121),)),
    ):
        for t in range(rows):
            for first, count, offset in runs:
                out[t * blocks + first : t * blocks + first + count, :] = acc_ref[
                    pl.ds(offset + t, count, stride=rows), :
                ]


def owner_kernel(list_ref, own_ref, minus_ref, left_ref, mid_ref, right_ref, plus_ref, out_ref):
    out_ref[...] = own_ref[...]
    middle = (left_ref, mid_ref, right_ref)
    for x in range(3):
        for y in range(3):
            for z in range(3):
                cell = (x * 3 + y) * 3 + z
                if cell == 13:
                    continue
                face = middle[x].at[z, 1] if y == 1 else (minus_ref if y == 0 else plus_ref).at[z, x]
                k = cell if cell < 13 else cell - 1
                for a in range(2):
                    rows = pl.ds(list_ref[a, k], ROWS, stride=OWN)
                    out_ref[rows, :] = out_ref[rows, :] + face[a].astype(F32)


def pair_kernel(keep_ref, received_ref, out_hbm, out_ref, sems):
    copies = []
    for i in range(4):
        part = pl.ds(i * 16, 16)
        out_ref[part] = keep_ref[part] + received_ref[part]
        copies.append(pltpu.make_async_copy(out_ref.at[part], out_hbm.at[part], sems.at[i]))
        copies[-1].start()
    for copy in copies:
        copy.wait()


def call(kernel, outs, scratch=(), scalars=0, inputs=0, flops=0, moved=0, vmem=16, copies=0, alias=()):
    specs = [pl.BlockSpec(memory_space=pltpu.SMEM)] * scalars
    specs += [pl.BlockSpec(memory_space=pltpu.VMEM)] * inputs
    return pl.pallas_call(
        kernel,
        out_shape=[jax.ShapeDtypeStruct(s, d) for s, d in outs],
        in_specs=specs,
        out_specs=[pl.BlockSpec(memory_space=pltpu.HBM if copies and i == 0 else pltpu.VMEM)
                   for i in range(len(outs))],
        scratch_shapes=[pltpu.VMEM(s, d) for s, d in scratch]
        + ([pltpu.SemaphoreType.DMA((copies,))] if copies else []),
        compiler_params=pltpu.CompilerParams(vmem_limit_bytes=vmem * MIB),
        cost_estimate=pl.CostEstimate(flops=flops, bytes_accessed=moved, transcendentals=0),
        input_output_aliases=dict(alias),
    )


def shift(value, axis, step):
    count = lax.axis_size(axis)
    return lax.ppermute(value, axis, [(i, (i + step) % count) for i in range(count)])


AXES = ("gx", "gyx", "gyc", "gz")
GY = ("gyx", "gyc")
FACE = (3, 3, 2, ROWS, C)


def regroup(parts, index, axis):
    return jnp.stack([lax.index_in_dim(p, index, axis, keepdims=False) for p in parts], 1)


def by_component(atoms):
    return atoms.transpose(1, 0, 2).reshape(ROWS * OWN, C)


def by_atom(rows):
    return rows.reshape(ROWS, OWN, C).transpose(1, 0, 2)


ORDERS = [((896, EPAD), BF16), ((768, 2 * EPAD), BF16), ((640, 2 * EPAD), BF16)]


def body(coefficients, send_list, sources, targets, wigner, edge_weight, cotangent, w_zero, w_one, w_two):
    listed = send_list.T
    src = sources.reshape(1, EDGES)
    tgt = targets.reshape(1, EDGES)
    ew = edge_weight.reshape(1, EDGES)
    core = lax.axis_index("gyc").astype(jnp.int32).reshape(1)
    coef = by_component(coefficients)

    z_minus, z_mid, z_plus = call(
        pick_kernel, [(FACE, BF16)] * 3, [((ROWS * OWN, C), F32)], scalars=1, inputs=1
    )(listed, coef)
    by_z = (shift(z_plus, "gz", 1), z_mid, shift(z_minus, "gz", -1))
    wt, q0, q1, q2 = call(
        q_kernel,
        [((456, EPAD), F32), ((EPAD, 896), BF16), ((512, 1536), BF16), ((512, 1280), BF16)],
        [((EPAD, 455), BF16), ((OWN, EPAD), BF16), ((8, EPAD), F32),
         ((13 * OWN, EPAD), BF16), ((3712, EPAD), BF16)],
        inputs=4, flops=2 * 10**9, moved=8 * 10**6,
    )(wigner, tgt, ew, by_component(cotangent))

    first, last, q0, q1, q2 = lax.optimization_barrier((by_z[0], by_z[2], q0, q1, q2))
    by_z = (first, z_mid, last)
    by_y = (
        shift(regroup(by_z, 2, 1), GY, 1), regroup(by_z, 1, 1), shift(regroup(by_z, 0, 1), GY, -1)
    )
    (dv,) = call(
        dv_kernel, [((PAIRS * EPAD, C), BF16)], inputs=6,
        flops=3 * 10**9, moved=16 * 10**6,
    )(q0, q1, q2, w_zero, w_one, w_two)

    own, g_minus, g_mid, g_plus = call(
        back_kernel,
        [((ROWS * OWN, C), F32)] + [(FACE, BF16)] * 3,
        [((TAB, EPAD), BF16), ((13 * TAB, 5 * EPAD), BF16), ((ROWS * TAB, C), F32)],
        vmem=11, inputs=3, flops=3 * 10**9, moved=12 * 10**6,
    )(dv, wt, src)
    first, last, g_minus, g_plus = lax.optimization_barrier((by_y[0], by_y[2], g_minus, g_plus))
    by_y = (first, by_y[1], last)
    take_x = lambda i: jnp.stack([p[i] for p in by_y], 0)
    left, mid, right = shift(take_x(2), "gx", 1), take_x(1), shift(take_x(0), "gx", -1)

    by_z = (shift(g_plus, "gz", 1), g_mid, shift(g_minus, "gz", -1))
    v0, v1, v2 = call(
        v_kernel,
        ORDERS,
        [((TAB, EPAD), BF16), (((TAB - OWN) * PITCH, C), F32), ((ROWS * TAB, C), BF16),
         ((13 * TAB, EPAD), BF16)],
        inputs=6, flops=3 * 10**9, moved=8 * 10**6, vmem=12,
    )(coef, left, mid, right, wt, src)

    first, last, v0, v1, v2 = lax.optimization_barrier((by_z[0], by_z[2], v0, v1, v2))
    by_z = (first, g_mid, last)
    back_x = lambda x: jnp.stack([p[x] for p in by_z], 0)
    by_x = (shift(back_x(2), "gx", 1), back_x(1), shift(back_x(0), "gx", -1))
    keep, send = call(
        grad_kernel,
        [((64, PIECE, C), BF16)] * 2,
        [((len(BLOCKS), TALL, C), F32)],
        scalars=1, inputs=6, flops=4 * 10**9, moved=24 * 10**6, vmem=26,
    )(core, v0, v1, v2, q0, q1, q2)
    first, last, keep, send = lax.optimization_barrier((by_x[0], by_x[2], keep, send))
    by_x = (first, by_x[1], last)
    received = shift(send, "gyc", 1)
    back_y = lambda y: regroup(by_x, y, 1)
    b_minus, b_plus = shift(back_y(2), GY, 1), shift(back_y(0), GY, -1)
    (pair,) = call(
        pair_kernel,
        [((64, PIECE, C), BF16)],
        [((64, PIECE, C), BF16)],
        copies=4, inputs=2, flops=10**7, moved=10**7, vmem=12,
    )(keep, received)
    pair, b_minus, b_plus = lax.optimization_barrier((pair, b_minus, b_plus))
    pieces = lax.all_to_all(pair, ("gx", "gyx", "gz"), 0, 0, tiled=False)

    (updated,) = call(
        u_kernel,
        [((ROWS * OWN, C), BF16)],
        [((OWN, EPAD), BF16), ((C, EPAD), F32), ((2 * EPAD, 896), BF16),
         ((PAIRS * EPAD, C), BF16), ((13 * OWN, 5 * EPAD), BF16)],
        inputs=9, flops=4 * 10**9, moved=20 * 10**6,
    )(v0, v1, v2, ew, tgt, wt, w_zero, w_one, w_two)
    (gradient,) = call(
        owner_kernel, [((ROWS * OWN, C), F32)], scalars=1, inputs=6, alias=((1, 0),), vmem=10
    )(
        listed, own, b_minus, *by_x, b_plus
    )
    zero, one, two = call(
        total_kernel,
        [((49, C), F32), ((72, C), F32), ((50, C), F32)],
        [((PIECE, C), F32)],
        inputs=1, flops=10**7, moved=4 * 10**6,
    )(pieces)
    return by_atom(updated), by_atom(gradient), zero.reshape(-1), one.reshape(-1), two.reshape(-1)


def solution(mesh):
    gx, gy, gz = mesh.devices.shape
    split = Mesh(mesh.devices.reshape(gx, gy // 2, 2, gz), AXES)
    lead = lambda rank: P(AXES, *([None] * (rank - 1)))
    in_specs = (lead(3), lead(2), lead(1), lead(1), lead(2), lead(1), lead(3), P(), P(), P())
    out_specs = (lead(3), lead(3), lead(1), lead(1), lead(1))
    return jax.shard_map(body, mesh=split, in_specs=in_specs, out_specs=out_specs, check_vma=False)
```

```python
import functools

import jax
import jax.numpy as jnp
from jax import lax
from jax.experimental import pallas as pl
from jax.experimental.pallas import tpu as pltpu
from jax.sharding import Mesh
from jax.sharding import PartitionSpec as P

F32 = jnp.float32
BF16 = jnp.bfloat16

LMAX = 6
ROWS = 49
C = 128
OWN = 16
CELLS = 54
TAB = 80
EDGES = 208
EPAD = 256
PITCH = 56
STARTS = [0, 1, 10, 35, 84, 165, 286, 455]

KEPT = [list(range(-min(l, 2), min(l, 2) + 1)) for l in range(LMAX + 1)]
PAIR_AT = {}
for _l in range(LMAX + 1):
    for _m in KEPT[_l]:
        PAIR_AT[(_l, _m)] = len(PAIR_AT)
PAIRS = len(PAIR_AT)
FIRST = {0: 0, 1: 7, -1: 13, 2: 19, -2: 24}


def order_block(l, m):
    return FIRST[m] + l - abs(m)


PIECE = 176
MIB = 1024 * 1024
GROUPED = 56


def nt(left, right):
    return lax.dot_general(left, right, (((1,), (1,)), ((), ())), preferred_element_type=F32)


def mm(left, right):
    return jnp.dot(left, right, preferred_element_type=F32)


def eye(rows, columns, dtype=BF16):
    a = lax.broadcasted_iota(jnp.int32, (rows, columns), 0)
    b = lax.broadcasted_iota(jnp.int32, (rows, columns), 1)
    return (a == b).astype(F32).astype(dtype)


def one_hot_rows(index_row, rows, out_ref):
    a = lax.broadcasted_iota(jnp.int32, (rows, EDGES), 0)
    out_ref[...] = jnp.zeros(out_ref.shape, out_ref.dtype)
    out_ref[:, :EDGES] = (a == index_row).astype(F32).astype(BF16)


def slots_of(sources_row):
    return sources_row + jnp.where(sources_row >= OWN + 26, 2, 0)


def fill_masked(wt_ref, hot_ref, l, m, out_ref, column):
    rows = hot_ref.shape[0]
    width = 2 * l + 1
    for j in range(width):
        at = STARTS[l] + (l + m) * width + j
        row = jnp.broadcast_to(wt_ref[at : at + 1, :], (16, EPAD)).astype(BF16)
        for g in range(0, rows, 16):
            out_ref[j * rows + g : j * rows + g + 16, column : column + EPAD] = (
                hot_ref[g : g + 16, :] * row
            )


def transposed_tables(perm_ref, slots):
    unit = eye(C, C)
    return [
        nt(unit, perm_ref[l * l * slots : (l + 1) * (l + 1) * slots, :]).astype(BF16)
        for l in range(LMAX + 1)
    ]


def pick_kernel(list_ref, coef_ref, minus_ref, mid_ref, plus_ref, flat_ref):
    flat_ref[: ROWS * OWN, :] = coef_ref[...].astype(F32)
    outs = (minus_ref, mid_ref, plus_ref)
    for x in range(3):
        for y in range(3):
            for z in range(3):
                cell = (x * 3 + y) * 3 + z
                for a in range(2):
                    if cell == 13:
                        outs[z][x, y, a] = jnp.zeros((ROWS, C), BF16)
                    else:
                        k = cell if cell < 13 else cell - 1
                        outs[z][x, y, a] = flat_ref[
                            pl.ds(list_ref[a, k], ROWS, stride=OWN), :
                        ].astype(BF16)


def q_kernel(wig_ref, tgt_ref, ew_ref, cot_ref, wt_ref, q0_ref, q1_ref, q2_ref,
             pad_ref, hot_ref, ewr_ref, a_ref, qt_ref):
    pad_ref[...] = jnp.zeros(pad_ref.shape, BF16)
    pad_ref[:EDGES, :] = wig_ref[...]
    wt_ref[...] = nt(eye(456, 455), pad_ref[...])
    one_hot_rows(tgt_ref[...], OWN, hot_ref)
    ewr_ref[...] = jnp.zeros(ewr_ref.shape, F32)
    ewr_ref[:, :EDGES] = jnp.broadcast_to(ew_ref[...], (8, EDGES))
    tables = transposed_tables(cot_ref, OWN)
    scale = ewr_ref[0:1, :]
    for l in range(LMAX + 1):
        for m in KEPT[l]:
            fill_masked(wt_ref, hot_ref, l, m, a_ref, 0)
            q = mm(tables[l], a_ref[: (2 * l + 1) * OWN, :]) * scale
            b = order_block(l, m)
            qt_ref[b * C : (b + 1) * C, :] = q.astype(BF16)
    unit = eye(EPAD, EPAD)
    q0_ref[...] = nt(unit, qt_ref[0:896, :]).astype(BF16)
    for out, start, n in ((q1_ref, 896, 768), (q2_ref, 2432, 640)):
        plus = nt(unit, qt_ref[start : start + n, :]).astype(BF16)
        minus = nt(unit, qt_ref[start + n : start + 2 * n, :]).astype(BF16)
        out[0:EPAD, 0:n] = plus
        out[0:EPAD, n : 2 * n] = minus
        out[EPAD : 2 * EPAD, 0:n] = minus
        out[EPAD : 2 * EPAD, n : 2 * n] = -plus


def dv_kernel(q0_ref, q1_ref, q2_ref, w0_ref, w1_ref, w2_ref, dv_ref):
    def put(value, l, m):
        b = PAIR_AT[(l, m)]
        dv_ref[b * EPAD : (b + 1) * EPAD, :] = value.astype(BF16)

    for order, q_ref, w_ref in ((0, q0_ref, w0_ref), (1, q1_ref, w1_ref), (2, q2_ref, w2_ref)):
        blocks = 7 - order
        for k in range(0, blocks, 2):
            n = min(2, blocks - k)
            both = nt(q_ref[...], w_ref[k * C : (k + n) * C, :])
            for i in range(n):
                put(both[:EPAD, i * C : (i + 1) * C], order + k + i, order)
                if order > 0:
                    put(both[EPAD:, i * C : (i + 1) * C], order + k + i, -order)


def back_kernel(dv_ref, wt_ref, src_ref, own_ref, minus_ref, mid_ref, plus_ref,
                hot_ref, b_ref, sum_ref):
    one_hot_rows(slots_of(src_ref[...]), TAB, hot_ref)
    for l in range(LMAX + 1):
        rows = (2 * l + 1) * TAB
        for i, m in enumerate(KEPT[l]):
            fill_masked(wt_ref, hot_ref, l, m, b_ref, i * EPAD)
        n = len(KEPT[l])
        first = PAIR_AT[(l, KEPT[l][0])] * EPAD
        sum_ref[l * l * TAB : l * l * TAB + rows, :] = mm(
            b_ref[:rows, : n * EPAD], dv_ref[first : first + n * EPAD, :]
        )
    for j in range(ROWS):
        own_ref[j * OWN : (j + 1) * OWN, :] = sum_ref[j * TAB : j * TAB + OWN, :]
    outs = (minus_ref, mid_ref, plus_ref)
    for x in range(3):
        for y in range(3):
            for z in range(3):
                for a in range(2):
                    s = OWN + ((x * 3 + y) * 3 + z) * 2 + a
                    outs[z][x, y, a] = sum_ref[pl.ds(s, ROWS, stride=TAB), :].astype(BF16)


def v_kernel(coef_ref, left_ref, mid_ref, right_ref, wt_ref, src_ref, v0_ref, v1_ref, v2_ref,
             hot_ref, flat_ref, perm_ref, b_ref):
    one_hot_rows(slots_of(src_ref[...]), TAB, hot_ref)
    ins = (left_ref, mid_ref, right_ref)
    for x in range(3):
        for y in range(3):
            for z in range(3):
                for a in range(2):
                    s = ((x * 3 + y) * 3 + z) * 2 + a
                    flat_ref[s * PITCH : s * PITCH + ROWS, :] = ins[x][y, z, a].astype(F32)
    flat_ref[CELLS * PITCH :, :] = jnp.zeros(((TAB - OWN - CELLS) * PITCH, C), F32)
    for j in range(ROWS):
        perm_ref[j * TAB : j * TAB + OWN, :] = coef_ref[j * OWN : (j + 1) * OWN, :]
        perm_ref[j * TAB + OWN : (j + 1) * TAB, :] = flat_ref[
            pl.ds(j, TAB - OWN, stride=PITCH), :
        ].astype(BF16)
    tables = transposed_tables(perm_ref, TAB)
    outs = {0: v0_ref, 1: v1_ref, 2: v2_ref}
    for l in range(LMAX + 1):
        for m in KEPT[l]:
            fill_masked(wt_ref, hot_ref, l, m, b_ref, 0)
            v = mm(tables[l], b_ref[: (2 * l + 1) * TAB, :]).astype(BF16)
            k = (l - abs(m)) * C
            column = EPAD if m < 0 else 0
            outs[abs(m)][k : k + C, column : column + EPAD] = v


ORDER_ROWS = {0: 7, 1: 6, 2: 5}
BLOCKS = [(0, k) for k in range(7)] + [(1, k) for k in range(12)] + [(2, k) for k in range(10)]
LEAD = 8
TALL = 912


def grad_kernel(core_ref, v0_ref, v1_ref, v2_ref, q0_ref, q1_ref, q2_ref, keep_ref, send_ref, g_ref):
    v_refs = (v0_ref, v1_ref, v2_ref)
    q_refs = (q0_ref, q1_ref, q2_ref)
    blocks = BLOCKS
    i = 0
    while i < len(blocks):
        order, k = blocks[i]
        n = 2 if i + 1 < len(blocks) and blocks[i + 1][0] == order else 1
        g = mm(v_refs[order][...], q_refs[order][:, k * C : (k + n) * C])
        rows = g.shape[0]
        for t in range(n):
            g_ref[i + t, LEAD : LEAD + rows, :] = g[:, t * C : (t + 1) * C]
        i += n
    source = []
    for i, (order, _) in enumerate(blocks):
        source += [(i, order, t) for t in range(ORDER_ROWS[order])]
    while len(source) < PIECE:
        i, order, t = source[-1]
        source.append((i, order, t + 1))
    place = lax.broadcasted_iota(jnp.int32, (8, C), 0)
    core = core_ref[0]

    def eight(p, first):
        value = None
        last = None
        for s in range(8):
            i, order, t = source[first + s]
            if i == last:
                continue
            last = i
            start = p * ORDER_ROWS[order] + (LEAD + t - s)
            rows = g_ref[i, pl.ds(start, 8), :]
            value = rows if value is None else jnp.where(place >= s, rows, value)
        return value

    def one(d, _):
        for h, out in ((0, keep_ref), (1, send_ref)):
            p = (d // 4) * 8 + (core ^ h) * 4 + d % 4
            for r in range(0, PIECE, 16):
                out[d, r : r + 16, :] = jnp.concatenate(
                    [eight(p, r), eight(p, r + 8)], 0
                ).astype(BF16)
        return 0

    lax.fori_loop(0, 64, one, 0, unroll=2)


def u_kernel(v0_ref, v1_ref, v2_ref, ew_ref, tgt_ref, wt_ref, w0_ref, w1_ref, w2_ref, out_ref,
             hot_ref, ewr_ref, v_ref, u_ref, a_ref):
    one_hot_rows(tgt_ref[...], OWN, hot_ref)
    ewr_ref[...] = jnp.zeros(ewr_ref.shape, F32)
    ewr_ref[:, :EDGES] = jnp.broadcast_to(ew_ref[...], (C, EDGES))
    scale = ewr_ref[...].T
    unit = eye(EPAD, EPAD)

    def put(value, l, m):
        b = PAIR_AT[(l, m)]
        u_ref[b * EPAD : (b + 1) * EPAD, :] = (value * scale).astype(BF16)

    v_ref[:EPAD, :] = nt(unit, v0_ref[...]).astype(BF16)
    for k in range(0, 7, 2):
        n = min(2, 7 - k)
        u0 = mm(v_ref[:EPAD, :], w0_ref[:, k * C : (k + n) * C])
        for i in range(n):
            put(u0[:, i * C : (i + 1) * C], k + i, 0)
    for order, vt_ref, w_ref in ((1, v1_ref, w1_ref), (2, v2_ref, w2_ref)):
        n = vt_ref.shape[0]
        v_ref[:EPAD, :n] = nt(unit, vt_ref[:, :EPAD]).astype(BF16)
        v_ref[EPAD:, :n] = nt(unit, vt_ref[:, EPAD:]).astype(BF16)
        v = v_ref[:, :n]
        for k in range(0, 7 - order, 2):
            c = min(2, 7 - order - k)
            real = mm(v, w_ref[:, k * C : (k + c) * C])
            imag = mm(v, w_ref[:, n + k * C : n + (k + c) * C])
            plus = real[:EPAD] - imag[EPAD:]
            minus = real[EPAD:] + imag[:EPAD]
            for i in range(c):
                put(plus[:, i * C : (i + 1) * C], order + k + i, order)
                put(minus[:, i * C : (i + 1) * C], order + k + i, -order)
    for l in range(LMAX + 1):
        rows = (2 * l + 1) * OWN
        for i, m in enumerate(KEPT[l]):
            fill_masked(wt_ref, hot_ref, l, m, a_ref, i * EPAD)
        n = len(KEPT[l])
        first = PAIR_AT[(l, KEPT[l][0])] * EPAD
        out_ref[l * l * OWN : l * l * OWN + rows, :] = mm(
            a_ref[:rows, : n * EPAD], u_ref[first : first + n * EPAD, :]
        ).astype(BF16)


def total_kernel(in_ref, zero_ref, one_ref, two_ref, acc_ref):
    def add(d, total):
        return total + in_ref[d].astype(F32)

    acc_ref[:PIECE, :] = lax.fori_loop(1, 64, add, in_ref[0].astype(F32), unroll=7)
    for out, rows, blocks, runs in (
        (zero_ref, 7, 7, ((0, 7, 0),)),
        (one_ref, 6, 12, ((0, 12, 49),)),
        (two_ref, 5, 10, ((0, 10, 121),)),
    ):
        for t in range(rows):
            for first, count, offset in runs:
                out[t * blocks + first : t * blocks + first + count, :] = acc_ref[
                    pl.ds(offset + t, count, stride=rows), :
                ]


def owner_kernel(list_ref, own_ref, minus_ref, left_ref, mid_ref, right_ref, plus_ref, out_ref, sum_ref):
    sum_ref[: ROWS * OWN, :] = own_ref[...]
    middle = (left_ref, mid_ref, right_ref)
    for x in range(3):
        for y in range(3):
            for z in range(3):
                cell = (x * 3 + y) * 3 + z
                if cell == 13:
                    continue
                face = middle[x].at[z, 1] if y == 1 else (minus_ref if y == 0 else plus_ref).at[z, x]
                k = cell if cell < 13 else cell - 1
                for a in range(2):
                    rows = pl.ds(list_ref[a, k], ROWS, stride=OWN)
                    sum_ref[rows, :] = sum_ref[rows, :] + face[a].astype(F32)
    out_ref[...] = sum_ref[: ROWS * OWN, :]


def pair_kernel(keep_ref, received_ref, out_hbm, out_ref, sems):
    copies = []
    for i in range(4):
        part = pl.ds(i * 16, 16)
        out_ref[part] = keep_ref[part] + received_ref[part]
        copies.append(pltpu.make_async_copy(out_ref.at[part], out_hbm.at[part], sems.at[i]))
        copies[-1].start()
    for copy in copies:
        copy.wait()


def call(kernel, outs, scratch=(), scalars=0, inputs=0, flops=0, moved=0, vmem=16, copies=0, alias=()):
    specs = [pl.BlockSpec(memory_space=pltpu.SMEM)] * scalars
    specs += [pl.BlockSpec(memory_space=pltpu.VMEM)] * inputs
    return pl.pallas_call(
        kernel,
        out_shape=[jax.ShapeDtypeStruct(s, d) for s, d in outs],
        in_specs=specs,
        out_specs=[pl.BlockSpec(memory_space=pltpu.HBM if copies and i == 0 else pltpu.VMEM)
                   for i in range(len(outs))],
        scratch_shapes=[pltpu.VMEM(s, d) for s, d in scratch]
        + ([pltpu.SemaphoreType.DMA((copies,))] if copies else []),
        compiler_params=pltpu.CompilerParams(vmem_limit_bytes=vmem * MIB),
        cost_estimate=pl.CostEstimate(flops=flops, bytes_accessed=moved, transcendentals=0),
        input_output_aliases=dict(alias),
    )


def shift(value, axis, step):
    count = lax.axis_size(axis)
    return lax.ppermute(value, axis, [(i, (i + step) % count) for i in range(count)])


AXES = ("gx", "gyx", "gyc", "gz")
GY = ("gyx", "gyc")
FACE = (3, 3, 2, ROWS, C)


def regroup(parts, index, axis):
    return jnp.stack([lax.index_in_dim(p, index, axis, keepdims=False) for p in parts], 1)


def by_component(atoms):
    return atoms.transpose(1, 0, 2).reshape(ROWS * OWN, C)


def by_atom(rows):
    return rows.reshape(ROWS, OWN, C).transpose(1, 0, 2)


ORDERS = [((896, EPAD), BF16), ((768, 2 * EPAD), BF16), ((640, 2 * EPAD), BF16)]


def body(coefficients, send_list, sources, targets, wigner, edge_weight, cotangent, w_zero, w_one, w_two):
    listed = send_list.T
    src = sources.reshape(1, EDGES)
    tgt = targets.reshape(1, EDGES)
    ew = edge_weight.reshape(1, EDGES)
    core = lax.axis_index("gyc").astype(jnp.int32).reshape(1)
    coef = by_component(coefficients)

    z_minus, z_mid, z_plus = call(
        pick_kernel, [(FACE, BF16)] * 3, [((GROUPED * OWN, C), F32)], scalars=1, inputs=1
    )(listed, coef)
    by_z = (shift(z_plus, "gz", 1), z_mid, shift(z_minus, "gz", -1))
    wt, q0, q1, q2 = call(
        q_kernel,
        [((456, EPAD), F32), ((EPAD, 896), BF16), ((512, 1536), BF16), ((512, 1280), BF16)],
        [((EPAD, 455), BF16), ((OWN, EPAD), BF16), ((8, EPAD), F32),
         ((13 * OWN, EPAD), BF16), ((3712, EPAD), BF16)],
        inputs=4, flops=2 * 10**9, moved=8 * 10**6,
    )(wigner, tgt, ew, by_component(cotangent))

    first, last, q0, q1, q2 = lax.optimization_barrier((by_z[0], by_z[2], q0, q1, q2))
    by_z = (first, z_mid, last)
    by_y = (
        shift(regroup(by_z, 2, 1), GY, 1), regroup(by_z, 1, 1), shift(regroup(by_z, 0, 1), GY, -1)
    )
    (dv,) = call(
        dv_kernel, [((PAIRS * EPAD, C), BF16)], inputs=6,
        flops=3 * 10**9, moved=16 * 10**6,
    )(q0, q1, q2, w_zero, w_one, w_two)

    own, g_minus, g_mid, g_plus = call(
        back_kernel,
        [((ROWS * OWN, C), F32)] + [(FACE, BF16)] * 3,
        [((TAB, EPAD), BF16), ((13 * TAB, 5 * EPAD), BF16), ((GROUPED * TAB, C), F32)],
        vmem=11, inputs=3, flops=3 * 10**9, moved=12 * 10**6,
    )(dv, wt, src)
    first, last, g_minus, g_plus = lax.optimization_barrier((by_y[0], by_y[2], g_minus, g_plus))
    by_y = (first, by_y[1], last)
    take_x = lambda i: jnp.stack([p[i] for p in by_y], 0)
    left, mid, right = shift(take_x(2), "gx", 1), take_x(1), shift(take_x(0), "gx", -1)

    by_z = (shift(g_plus, "gz", 1), g_mid, shift(g_minus, "gz", -1))
    v0, v1, v2 = call(
        v_kernel,
        ORDERS,
        [((TAB, EPAD), BF16), (((TAB - OWN) * PITCH, C), F32), ((ROWS * TAB, C), BF16),
         ((13 * TAB, EPAD), BF16)],
        inputs=6, flops=3 * 10**9, moved=8 * 10**6, vmem=12,
    )(coef, left, mid, right, wt, src)

    first, last, v0, v1, v2 = lax.optimization_barrier((by_z[0], by_z[2], v0, v1, v2))
    by_z = (first, g_mid, last)
    back_x = lambda x: jnp.stack([p[x] for p in by_z], 0)
    by_x = (shift(back_x(2), "gx", 1), back_x(1), shift(back_x(0), "gx", -1))
    keep, send = call(
        grad_kernel,
        [((64, PIECE, C), BF16)] * 2,
        [((len(BLOCKS), TALL, C), F32)],
        scalars=1, inputs=6, flops=4 * 10**9, moved=24 * 10**6, vmem=26,
    )(core, v0, v1, v2, q0, q1, q2)
    first, last, keep, send = lax.optimization_barrier((by_x[0], by_x[2], keep, send))
    by_x = (first, by_x[1], last)
    received = shift(send, "gyc", 1)
    back_y = lambda y: regroup(by_x, y, 1)
    b_minus, b_plus = shift(back_y(2), GY, 1), shift(back_y(0), GY, -1)
    (pair,) = call(
        pair_kernel,
        [((64, PIECE, C), BF16)],
        [((64, PIECE, C), BF16)],
        copies=4, inputs=2, flops=10**7, moved=10**7, vmem=12,
    )(keep, received)
    pair, b_minus, b_plus = lax.optimization_barrier((pair, b_minus, b_plus))
    pieces = lax.all_to_all(pair, ("gx", "gyx", "gz"), 0, 0, tiled=False)

    (updated,) = call(
        u_kernel,
        [((ROWS * OWN, C), BF16)],
        [((OWN, EPAD), BF16), ((C, EPAD), F32), ((2 * EPAD, 896), BF16),
         ((PAIRS * EPAD, C), BF16), ((13 * OWN, 5 * EPAD), BF16)],
        inputs=9, flops=4 * 10**9, moved=20 * 10**6,
    )(v0, v1, v2, ew, tgt, wt, w_zero, w_one, w_two)
    (gradient,) = call(
        owner_kernel, [((ROWS * OWN, C), F32)], [((GROUPED * OWN, C), F32)], scalars=1, inputs=6, alias=((1, 0),), vmem=10
    )(
        listed, own, b_minus, *by_x, b_plus
    )
    zero, one, two = call(
        total_kernel,
        [((49, C), F32), ((72, C), F32), ((50, C), F32)],
        [((PIECE + 32, C), F32)],
        inputs=1, flops=10**7, moved=4 * 10**6,
    )(pieces)
    return by_atom(updated), by_atom(gradient), zero.reshape(-1), one.reshape(-1), two.reshape(-1)


def solution(mesh):
    gx, gy, gz = mesh.devices.shape
    split = Mesh(mesh.devices.reshape(gx, gy // 2, 2, gz), AXES)
    lead = lambda rank: P(AXES, *([None] * (rank - 1)))
    in_specs = (lead(3), lead(2), lead(1), lead(1), lead(2), lead(1), lead(3), P(), P(), P())
    out_specs = (lead(3), lead(3), lead(1), lead(1), lead(1))
    return jax.shard_map(body, mesh=split, in_specs=in_specs, out_specs=out_specs, check_vma=False)
```
